512 devices in a mesh: grp: 32 (over x, z), seq: 16 (over y, core).
Axes of the slice: x: 4, y: 8, z: 8, core: 2. Of those that a mesh axis runs over, the one named last changes fastest.
Arguments:
- query_rows: bfloat16 [512, 128, 1536], P(('grp', 'seq')), may hold values from -400 to 400
- key_rows: bfloat16 [512, 128, 1536], P(('grp', 'seq')), may hold values from -400 to 400
- value_rows: bfloat16 [512, 128, 1536], P(('grp', 'seq')), may hold values from -6 to 6
- out_grad: bfloat16 [512, 128, 1536], P(('grp', 'seq')), may hold values from -6 to 6
- proj_grad: bfloat16 [512, 3072, 128], P('grp', 'seq'), may hold values from -6 to 6
- proj_weight: bfloat16 [3072, 1536], P('seq'), may hold values from -0.15625 to 0.15625
- query_gain: float32 [1536], P('grp'), may hold values from 0.5 to 5
- key_gain: float32 [1536], P('grp'), may hold values from 0.5 to 5
- clip_of_frame: int32 [512], replicated, may hold values from 0 to 63, never falling along the last dimension, each value on 1 to 16 neighbouring positions
- patch_count: int32 [64], replicated, may hold values from 1 to 128, as said below
Outputs:
- attended: bfloat16 [512, 128, 1536], P(('grp', 'seq'))
- projected: bfloat16 [512, 3072, 128], P('grp', 'seq')
- query_grad: bfloat16 [512, 128, 1536], P(('grp', 'seq'))
- key_grad: bfloat16 [512, 128, 1536], P(('grp', 'seq'))
- value_grad: bfloat16 [512, 128, 1536], P(('grp', 'seq'))
- weight_grad: float32 [1536, 3072], P('grp', 'seq')
- query_gain_grad: float32 [1536], P('grp')
- key_gain_grad: float32 [1536], P('grp')
The draws below stay inside these ranges and needn't reach their ends.
Inputs may be any that keep to these rules, and one draw needn't show every extreme that they name: `clip_of_frame`: the frames of a clip are consecutive; a clip has at most 16 frames, and some clip has exactly 16. `patch_count`: some clip has 128 live positions and some has 1.
All inputs are finite; a program needn't handle non-finite values.
Results may differ from the reference program's by a relative error of at most 0.039.
The reference program's roundings to bfloat16 on the way count: a program that leaves them out, or rounds other values in their place, can miss the bound.
Values may be sent and summed in bfloat16 or wider, within the bound.
A program may use at most 64 MiB of HBM per device.

```python
import math
import jax
import jax.numpy as jnp
import numpy as np
from jax import lax

HEADS = 12
HEAD_DIM = 128
D = 3072
CHANNELS = 1536
PATCHES = 128
GROUP_FRAMES = 16
FRAMES = 512
CLIPS = 64
TOKENS = 65536
N_GRP = 32


def query_values(key):
    first_key = jax.random.fold_in(key, 101)
    third_key = jax.random.fold_in(key, 103)
    fourth_key = jax.random.fold_in(key, 104)
    gauss = jnp.clip(jax.random.normal(first_key, (FRAMES, PATCHES, CHANNELS), jnp.float32), -4.0, 4.0)
    row_scale = jnp.exp(jax.random.uniform(third_key, (FRAMES, PATCHES, 1), jnp.float32, 0.0, 2.3))
    column_scale = jnp.exp(jax.random.uniform(fourth_key, (1, 1, CHANNELS), jnp.float32, 0.0, 2.3))
    return gauss * row_scale * column_scale


def draw_query_rows(key, part):
    values = query_values(key)
    return values.astype(jnp.bfloat16)


def draw_key_rows(key, part):
    key = jax.random.fold_in(key, 5)
    own_field = query_values(key)
    return own_field.astype(jnp.bfloat16)


def draw_query_gain(key, part):
    key = jax.random.fold_in(key, 11)
    values = jnp.exp(jax.random.uniform(key, (CHANNELS,), jnp.float32, -0.6931, 0.6931))
    return values


def draw_key_gain(key, part):
    key = jax.random.fold_in(key, 13)
    values = jnp.exp(jax.random.uniform(key, (CHANNELS,), jnp.float32, -0.6931, 0.6931))
    return values


def draw_patch_count(key, part):
    key = jax.random.fold_in(key, 17)
    values = jax.random.randint(key, (CLIPS,), 1, PATCHES + 1, jnp.int32)
    order = jax.random.permutation(jax.random.fold_in(key, 1), CLIPS)
    values = values.at[order[0]].set(PATCHES)
    values = values.at[order[1]].set(1)
    return values


def with_spikes(drawn, rng, source, target, shards_of, factor):
    def block_of(axis_at):
        return (jnp.arange(drawn.shape[axis_at]) // (drawn.shape[axis_at] // shards_of)).reshape((-1,) + (1,) * (drawn.ndim - 1 - axis_at))

    first = jax.random.permutation(rng, shards_of)[block_of(target)]
    second = (block_of(target) + shards_of // 2) % shards_of
    return jnp.where((block_of(source) == first) | (block_of(source) == second), factor * drawn, drawn)


def shard_levels(rng, extent, split, smallest, high):
    factor_of, own = 1.0, jax.random.fold_in(rng, 6)
    for dim, blocks in split:
        draws = jnp.exp(jax.random.uniform(jax.random.fold_in(own, dim), (blocks,), jnp.float32, smallest / len(split), high / len(split)))
        factor_of = factor_of * jnp.repeat(draws, extent[dim] // blocks).reshape([-1 if axis == dim else 1 for axis in range(len(extent))])
    return factor_of


def split_up(amount, total, limit, lean):
    loads = [(1 << 20) // math.isqrt(rank ** lean) + 1 for rank in range(2, amount + 1)]
    surplus, given = total - limit - (amount - 1), [1] * (amount - 1)
    while surplus > 0:
        candidates = [i for i in range(amount - 1) if given[i] < limit]
        mass, budget = sum([loads[i] for i in candidates]), surplus
        for i in candidates:
            more = min(limit - given[i], max(1, budget * loads[i] // mass), surplus)
            given[i] = given[i] + more
            surplus = surplus - more
    return np.array([limit] + given)


def uneven_parts(key, number_of, total, limit, skew):
    if number_of == 2:
        one = jax.random.randint(key, (), max(1, total - limit), min(limit, total - 1) + 1)
        return jnp.stack([one, total - one])
    tallies = jnp.asarray(split_up(number_of, total, limit, skew), jnp.int32)
    twos = (number_of - 1) // 2
    donor, taker = tallies[1:1 + 2 * twos:2], tallies[2:2 + 2 * twos:2]
    room = jnp.minimum(donor - 1, limit - taker)
    moved = jax.random.randint(jax.random.fold_in(key, 1), (twos,), 0, 1 << 20) % (room + 1)
    tallies = tallies.at[1:1 + 2 * twos:2].set(donor - moved).at[2:2 + 2 * twos:2].set(taker + moved)
    return tallies[jax.random.permutation(jax.random.fold_in(key, 2), number_of)]


def gaussian(stream_key, extent, scale, most, cuts=(), held_as=jnp.bfloat16):
    gain = shard_levels(stream_key, extent, cuts, -0.22, 0.18) if cuts else 1.0
    values = jax.random.normal(stream_key, extent, jnp.float32) * scale * gain
    return jnp.minimum(jnp.maximum(values, -most), most).astype(held_as)


def gaussian_with(rng, shape, scale, most, pieces, heavy, held_as=jnp.bfloat16):
    entries = scale * jax.random.normal(rng, shape, jnp.float32)
    if pieces:
        entries = entries * shard_levels(rng, shape, pieces, -0.22, 0.18)
    return jnp.clip(with_spikes(entries, jax.random.fold_in(rng, 3), *heavy), -most, most).astype(held_as)


def setup_inputs(seed: int = 0) -> dict:
    arg_keys = jax.random.split(jax.random.key(seed), 11)
    query_rows = draw_query_rows(jax.random.fold_in(arg_keys[10], 71), 0)
    key_rows = draw_key_rows(jax.random.fold_in(arg_keys[10], 71), 0)
    value_rows = gaussian(arg_keys[2], (FRAMES, PATCHES, CHANNELS), 1.0, 6.0, ((0, 512),))
    out_grad = gaussian(arg_keys[3], (FRAMES, PATCHES, CHANNELS), 1.0, 6.0, ((0, 512),))
    proj_grad = gaussian_with(arg_keys[4], (FRAMES, D, PATCHES), 1.0, 6.0, ((0, 32), (1, 16)), (0, 1, 32, 2.75))
    proj_weight = gaussian(arg_keys[5], (D, CHANNELS), CHANNELS ** -0.5, 0.15625, ((0, 16),))
    query_gain = draw_query_gain(jax.random.fold_in(arg_keys[10], 71), 0)
    key_gain = draw_key_gain(jax.random.fold_in(arg_keys[10], 71), 0)
    clip_of_frame = jnp.searchsorted(jnp.cumsum(uneven_parts(arg_keys[8], CLIPS, FRAMES, GROUP_FRAMES, 2)), jnp.arange(FRAMES), side="right").astype(jnp.int32)
    patch_count = draw_patch_count(jax.random.fold_in(arg_keys[10], 71), 0)
    return {"query_rows": query_rows, "key_rows": key_rows, "value_rows": value_rows, "out_grad": out_grad, "proj_grad": proj_grad, "proj_weight": proj_weight, "query_gain": query_gain, "key_gain": key_gain, "clip_of_frame": clip_of_frame, "patch_count": patch_count}


EPS = 1e-06
NEGATIVE = -1e+30

def head_norm(features, gain_row):
    shaped = features.astype(jnp.float32).reshape(features.shape[:-1] + (HEADS, HEAD_DIM))
    inverse = lax.rsqrt(lax.optimization_barrier(jnp.mean(shaped * shaped, axis=-1, keepdims=True)) + EPS)
    normed = (shaped * inverse).reshape(features.shape) * gain_row
    return (normed.astype(jnp.bfloat16), inverse)

def norm_backward(features, gain_row, inverse, upstream):
    shaped = features.astype(jnp.float32).reshape(features.shape[:-1] + (HEADS, HEAD_DIM))
    incoming = upstream.astype(jnp.float32)
    weighted = (incoming * gain_row).reshape(shaped.shape)
    along_head = lax.optimization_barrier(jnp.mean(weighted * shaped, axis=-1, keepdims=True))
    grad_rows = inverse * weighted - shaped * inverse * inverse * inverse * along_head
    gain_terms = incoming * (shaped * inverse).reshape(features.shape)
    gain_sum = lax.optimization_barrier(jnp.sum(gain_terms.reshape(-1, features.shape[-1]), axis=0))
    return (grad_rows.reshape(features.shape).astype(jnp.bfloat16), gain_sum)

def split_heads(values):
    return values.reshape(values.shape[:-1] + (HEADS, HEAD_DIM))

def product(pattern, first_operand, second_operand):
    return jnp.einsum(pattern, first_operand.astype(jnp.float32), second_operand.astype(jnp.float32))

def softmax_rows(scores, pair_mask, live_rows):
    masked = jnp.where(pair_mask, scores, NEGATIVE)
    row_top = lax.optimization_barrier(jnp.max(masked, axis=-1, keepdims=True))
    spread = jnp.where(pair_mask, jnp.exp(masked - row_top), 0.0)
    row_total = jnp.where(live_rows, lax.optimization_barrier(jnp.sum(spread, axis=-1, keepdims=True)), 1.0)
    return (spread / row_total, row_top + jnp.log(row_total))

def reference(query_rows, key_rows, value_rows, out_grad, proj_grad, proj_weight, query_gain, key_gain, clip_of_frame, patch_count):
    frames_group = GROUP_FRAMES
    score_scale = HEAD_DIM ** (-0.5)
    grad_flat = jnp.transpose(proj_grad, (0, 2, 1)).reshape(TOKENS, D)
    query_normed, query_inverse = head_norm(query_rows, query_gain)
    key_normed, key_inverse = head_norm(key_rows, key_gain)
    border = jnp.full((frames_group,), -1, jnp.int32)
    clip_padded = jnp.concatenate([border, clip_of_frame.astype(jnp.int32), border])
    clip_slots = jnp.arange(CLIPS, dtype=jnp.int32)
    counts = lax.optimization_barrier(jnp.sum(jnp.where(clip_padded[:, None] == clip_slots[None, :], patch_count[None, :], 0), axis=1))
    live_padded = jnp.arange(PATCHES, dtype=jnp.int32)[None, :] < counts[:, None]

    def pad_frames(values):
        widths = [(frames_group, frames_group)] + [(0, 0)] * (values.ndim - 1)
        return jnp.pad(values, widths)
    query_pad = split_heads(pad_frames(query_normed))
    key_pad = split_heads(pad_frames(key_normed))
    value_pad = split_heads(pad_frames(value_rows))
    grad_pad = split_heads(pad_frames(out_grad))

    def window(values, block_start, length):
        return lax.dynamic_slice_in_dim(values, block_start, length, 0)

    def first_pass(block_index):
        block_start = block_index * frames_group
        own_start = block_start + frames_group
        query_part = window(query_pad, own_start, frames_group)
        grad_part = window(grad_pad, own_start, frames_group)
        key_part = window(key_pad, block_start, 3 * frames_group)
        value_part = window(value_pad, block_start, 3 * frames_group)
        own_clip = window(clip_padded, own_start, frames_group)
        nearby_clip = window(clip_padded, block_start, 3 * frames_group)
        own_live = window(live_padded, own_start, frames_group).T
        pair_mask = ((own_clip[:, None] == nearby_clip[None, :])[None] & own_live[:, :, None])[:, None]
        live_rows = own_live[:, None, :, None]
        scores = product('qphe,kphe->phqk', query_part, key_part) * score_scale
        probabilities, log_total = softmax_rows(scores, pair_mask, live_rows)
        rounded = probabilities.astype(jnp.bfloat16)
        attended = product('phqk,kphe->qphe', rounded, value_part).astype(jnp.bfloat16)
        row_delta = product('qphe,qphe->phq', grad_part, attended)[..., None]
        prob_grad = product('qphe,kphe->phqk', grad_part, value_part)
        score_grad = (probabilities * (prob_grad - row_delta) * score_scale).astype(jnp.bfloat16)
        normed_grad = product('phqk,kphe->qphe', score_grad, key_part).astype(jnp.bfloat16)
        return (attended, normed_grad, jnp.transpose(log_total[..., 0], (2, 0, 1)), jnp.transpose(row_delta[..., 0], (2, 0, 1)))
    blocks = jnp.arange(N_GRP, dtype=jnp.int32)
    attended, query_side, log_total, row_delta = lax.map(first_pass, blocks)
    attended = attended.reshape(FRAMES, PATCHES, CHANNELS)
    query_side = query_side.reshape(FRAMES, PATCHES, CHANNELS)
    total_pad = pad_frames(log_total.reshape(FRAMES, PATCHES, HEADS))
    delta_pad = pad_frames(row_delta.reshape(FRAMES, PATCHES, HEADS))

    def second_pass(block_index):
        block_start = block_index * frames_group
        own_start = block_start + frames_group
        key_part = window(key_pad, own_start, frames_group)
        value_part = window(value_pad, own_start, frames_group)
        query_part = window(query_pad, block_start, 3 * frames_group)
        grad_part = window(grad_pad, block_start, 3 * frames_group)
        total_part = jnp.transpose(window(total_pad, block_start, 3 * frames_group), (1, 2, 0))[..., None]
        delta_part = jnp.transpose(window(delta_pad, block_start, 3 * frames_group), (1, 2, 0))[..., None]
        own_clip = window(clip_padded, own_start, frames_group)
        nearby_clip = window(clip_padded, block_start, 3 * frames_group)
        nearby_live = window(live_padded, block_start, 3 * frames_group).T
        pair_mask = ((nearby_clip[:, None] == own_clip[None, :])[None] & nearby_live[:, :, None])[:, None]
        scores = product('qphe,kphe->phqk', query_part, key_part) * score_scale
        probabilities = jnp.where(pair_mask, jnp.exp(jnp.where(pair_mask, scores - total_part, 0.0)), 0.0)
        rounded = probabilities.astype(jnp.bfloat16)
        value_side = product('phqk,qphe->kphe', rounded, grad_part).astype(jnp.bfloat16)
        prob_grad = product('qphe,kphe->phqk', grad_part, value_part)
        score_grad = (probabilities * (prob_grad - delta_part) * score_scale).astype(jnp.bfloat16)
        key_side = product('phqk,qphe->kphe', score_grad, query_part).astype(jnp.bfloat16)
        return (key_side, value_side)
    key_side, value_side = lax.map(second_pass, blocks)
    key_side = key_side.reshape(FRAMES, PATCHES, CHANNELS)
    value_grad = value_side.reshape(FRAMES, PATCHES, CHANNELS)
    query_grad, query_terms = norm_backward(query_rows, query_gain, query_inverse, query_side)
    key_grad, key_terms = norm_backward(key_rows, key_gain, key_inverse, key_side)
    token_root = TOKENS ** 0.5
    attended_flat = attended.reshape(TOKENS, CHANNELS)
    projected = product('tc,dc->td', attended_flat, proj_weight)
    projected = jnp.transpose(projected.astype(jnp.bfloat16).reshape(FRAMES, PATCHES, D), (0, 2, 1))
    weight_grad = product('tc,td->cd', attended_flat, grad_flat) / token_root
    return (attended, projected, query_grad, key_grad, value_grad, weight_grad, query_terms / token_root, key_terms / token_root)
```

```python
import functools

import jax
import jax.numpy as jnp
from jax import lax
from jax.experimental import pallas as pl
from jax.experimental.pallas import tpu as pltpu
from jax.sharding import PartitionSpec as P

HEADS = 12
HEAD_DIM = 128
EPS = 1e-06
NEGATIVE = -1e30
SCALE = HEAD_DIM ** (-0.5)
MESH = pl.DeviceIdType.MESH

POS = 16
CORES = 2
CHUNKS = 2
CHUNK_HEADS = HEADS // (CORES * CHUNKS)
CH = CHUNK_HEADS * HEAD_DIM
HALF = CHUNKS * CH
X = CORES * CHUNKS
BLOCK_POS = 4
LANES = 256
VMEM_LIMIT = 60 * 1024 * 1024


def dot(a, b, dims):
    return lax.dot_general(a, b, (dims, ((), ())), preferred_element_type=jnp.float32)


def place():
    seq_count = lax.axis_size("seq")
    group_count = lax.axis_size("grp")
    grp, seq = lax.axis_index("grp"), lax.axis_index("seq")
    z_count, y_count = group_count // X, seq_count // CORES
    return (
        grp, seq, z_count, y_count,
        lax.div(grp, z_count), lax.rem(grp, z_count),
        lax.div(seq, CORES), lax.rem(seq, CORES),
    )


def wait_bytes(ref, sem):
    pltpu.make_async_copy(ref, ref, sem).wait()


def remote(src, dst, send_sem, recv_sem, device):
    return pltpu.make_async_remote_copy(
        src_ref=src, dst_ref=dst, send_sem=send_sem, recv_sem=recv_sem, device_id=device, device_id_type=MESH
    )


def loop(low, high, step):
    def one(i, carry):
        step(i)
        return carry

    lax.fori_loop(low, high, one, 0)


def greet(with_neighbours):
    grp, seq, z_count, y_count, x, z, y, core = place()
    seq_count, group_count = y_count * CORES, z_count * X
    barrier = pltpu.get_barrier_semaphore()

    def signal(device):
        pl.semaphore_signal(barrier, inc=1, device_id=device, device_id_type=MESH)

    loop(1, seq_count, lambda d: signal({"seq": lax.rem(seq + d, seq_count)}))
    if z_count > 1:
        loop(1, z_count, lambda d: signal({"grp": x * z_count + lax.rem(z + d, z_count)}))
    loop(1, X, lambda d: signal({"grp": lax.rem(x + d, X) * z_count + z}))
    total = seq_count - 1 + z_count - 1 + X - 1
    if with_neighbours:
        signal({"grp": lax.rem(grp + 1, group_count)})
        signal({"grp": lax.rem(grp + group_count - 1, group_count)})
        total += 2
    pl.semaphore_wait(barrier, total)


def exchange_kernel(
    q, k, v, g, gain, win, full, stage, gz, gx, gs, load_sem, send_sem, recv_sem, halo_send, halo_recv, gain_send, gain_recv
):
    grp, seq, z_count, y_count, x, z, y, core = place()
    seq_count, group_count = y_count * CORES, z_count * X
    loads = [pltpu.make_async_copy(ref, stage.at[i], load_sem.at[i]) for i, ref in enumerate((q, k, v, g))]
    for load in loads:
        load.start()
    greet(True)
    if z_count > 1:
        loop(
            1, z_count,
            lambda d: remote(
                gain, gz.at[z], gain_send.at[0], gain_recv.at[0], {"grp": x * z_count + lax.rem(z + d, z_count)}
            ).start(),
        )
    for load in loads:
        load.wait()
    for c in range(CHUNKS):
        def send(i, c=c):
            odd = lax.rem(i, 2)
            dy = odd * lax.div(i + 1, 2) + (1 - odd) * (y_count - lax.div(i, 2))
            other = lax.rem(y + dy, y_count)
            for cc in range(CORES):
                remote(
                    stage.at[:, other, :, pl.ds(cc * HALF + c * CH, CH)], win.at[c, 0, :, seq],
                    send_sem.at[c], recv_sem.at[c], {"seq": other * CORES + cc},
                ).start()

        pltpu.make_async_copy(
            stage.at[:, y, :, pl.ds(pl.multiple_of(core * HALF + c * CH, HEAD_DIM), CH)],
            win.at[c, 0, :, seq], recv_sem.at[c],
        ).start()
        remote(
            stage.at[:, y, :, pl.ds(pl.multiple_of((1 - core) * HALF + c * CH, HEAD_DIM), CH)],
            win.at[c, 0, :, seq], send_sem.at[c], recv_sem.at[c], {"seq": y * CORES + 1 - core},
        ).start()
        loop(1, y_count, send)
    gz[z] = gain[...]
    if z_count > 1:
        wait_bytes(gz.at[pl.ds(0, z_count - 1)], gain_recv.at[0])
    gs[...] = jnp.sum(gz[...], axis=0)
    loop(
        1, X,
        lambda d: remote(
            gs, gx.at[x], gain_send.at[1], gain_recv.at[1], {"grp": lax.rem(x + d, X) * z_count + z}
        ).start(),
    )
    gx[x] = gs[...]
    wait_bytes(gx.at[pl.ds(0, X - 1)], gain_recv.at[1])
    full[...] = jnp.sum(gx[...], axis=0)
    halos = []
    for c in range(CHUNKS):
        wait_bytes(win.at[c, 0], recv_sem.at[c])
        for way, step in enumerate((1, group_count - 1)):
            halo = remote(
                win.at[c, 0], win.at[c, 1 + way], halo_send.at[c, way], halo_recv.at[c, way],
                {"grp": lax.rem(grp + step, group_count)},
            )
            halo.start()
            halos.append(halo)
    for halo in halos:
        halo.wait()
    for c in range(CHUNKS):
        wait_bytes(win.at[c, 0, :, pl.ds(0, seq_count - 1)], send_sem.at[c])
    if z_count > 1:
        wait_bytes(gz.at[pl.ds(0, z_count - 1)], gain_send.at[0])
    wait_bytes(gx.at[pl.ds(0, X - 1)], gain_send.at[1])


def mean_lanes(values):
    return jnp.mean(values, axis=-1, keepdims=True)


def attend(win, gain, code_col, code_row, limit, perm, unperm, base, ret, att, normed, held, bias, back):
    frames = win.shape[2]
    rows = frames * POS
    wide = BLOCK_POS * frames
    bias[...] = jnp.where(code_col[...] == code_row[...], 0.0, NEGATIVE)

    def gather(slot):
        for a in range(4):
            moved = dot(perm[...], win[slot, a].reshape(rows, CH), ((1,), (0,)))
            for h in range(CHUNK_HEADS):
                part = moved[:, h * HEAD_DIM : (h + 1) * HEAD_DIM]
                if a < 2:
                    inverse = lax.rsqrt(mean_lanes(part * part) + EPS)
                    part_normed = part * inverse * gain[a : a + 1, h * HEAD_DIM : (h + 1) * HEAD_DIM]
                    normed[a, h, slot] = part_normed.astype(jnp.bfloat16)

                    @pl.when(slot == 0)
                    def _():
                        held[a, h] = part
                else:
                    normed[a, h, slot] = part.astype(jnp.bfloat16)

    loop(0, 3, gather)
    totals = []
    for h in range(CHUNK_HEADS):
        lanes = slice(h * HEAD_DIM, (h + 1) * HEAD_DIM)

        def block(b, sums, h=h, lanes=lanes):
            at = pl.ds(pl.multiple_of(b * wide, wide), wide)
            query, key, value, grad = (normed[a, h, :, at, :].reshape(3 * wide, HEAD_DIM) for a in range(4))
            scores = dot(query, key, ((1,), (1,))) * SCALE + bias[...]
            prob_grad = dot(grad, value, ((1,), (1,)))
            spread = jnp.exp(scores - jnp.max(scores, axis=-1, keepdims=True))
            live = jnp.where(limit[...] > base + b * BLOCK_POS, 1.0, 0.0)
            probs = spread * (live / jnp.sum(spread, axis=-1, keepdims=True))
            rounded = probs.astype(jnp.bfloat16)
            attended = dot(rounded, value, ((1,), (0,))).astype(jnp.bfloat16)
            delta = jnp.sum(grad.astype(jnp.float32) * attended.astype(jnp.float32), axis=-1, keepdims=True)
            score_grad = (probs * (prob_grad - delta) * SCALE).astype(jnp.bfloat16)
            back[0, at, lanes] = attended[:wide]
            back[3, at, lanes] = dot(rounded[:, :wide], grad, ((0,), (0,))).astype(jnp.bfloat16)
            ups = (
                dot(score_grad[:wide], key, ((1,), (0,))),
                dot(score_grad[:, :wide], query, ((0,), (0,))),
            )
            new = []
            for a in range(2):
                up = ups[a].astype(jnp.bfloat16).astype(jnp.float32)
                rows_in = held[a, h, at, :]
                inverse = lax.rsqrt(mean_lanes(rows_in * rows_in) + EPS)
                weighted = up * gain[a : a + 1, lanes]
                along = mean_lanes(weighted * rows_in)
                scaled = rows_in * inverse
                back[1 + a, at, lanes] = (inverse * weighted - scaled * inverse * inverse * along).astype(jnp.bfloat16)
                new.append(sums[a] + jnp.sum(up * scaled, axis=0, keepdims=True))
            return tuple(new)

        zero = jnp.zeros((1, HEAD_DIM), jnp.float32)
        totals.append(lax.fori_loop(0, POS // BLOCK_POS, block, (zero, zero)))
    for a in range(4):
        out = dot(unperm[...], back[a], ((1,), (0,))).astype(jnp.bfloat16).reshape(frames, POS, CH)
        if a == 0:
            att[pl.ds(0, frames)] = out
        else:
            ret[a - 1] = out
    row = lax.broadcasted_iota(jnp.int32, (POS, CH), 0)
    packed = jnp.zeros((POS, CH), jnp.float32)
    for a in range(2):
        total = jnp.concatenate([sums[a] for sums in totals], axis=1)
        packed = packed + hi_lo(total, row, 2 * a)
    att[frames] = packed.astype(jnp.bfloat16)


def hi_lo(total, row, first):
    high = total.astype(jnp.bfloat16).astype(jnp.float32)
    low = total - high
    return jnp.where(row == first, high, 0.0) + jnp.where(row == first + 1, low, 0.0)


def attend_kernel(win, gain, code_col, code_row, limit, perm, unperm, ret, att, normed, held, bias, back):
    base = lax.div(lax.axis_index("seq"), CORES) * POS
    attend(
        win.at[0], gain, code_col, code_row, limit, perm, unperm, base, ret.at[0], att.at[0], normed, held, bias, back
    )


def collect_kernel(
    ret, att, grad, weight, rows_out, att_out, proj_out, wide_out, ag, acc, turn, zsend, zrecv, xsend, xrecv,
    ret_send, ret_recv, own_sem, ring_send, ring_recv, sib_send, sib_recv, z_send, z_recv, x_send, x_recv, att_sem,
):
    grp, seq, z_count, y_count, x, z, y, core = place()
    seq_count = y_count * CORES
    frames, width, patches = grad.shape
    far = y_count // 2
    share = CH // z_count
    half = (frames + 1) // 2
    halves = ((0, half), (half, frames + 1 - half))
    greet(False)
    neighbours = (lax.rem(y + 1, y_count) * CORES + core, lax.rem(y + y_count - 1, y_count) * CORES + core)
    sibling = y * CORES + 1 - core

    def ring_copy(c, way, hop, ref=None):
        at = lax.rem(y + hop * (y_count - 1 if way == 0 else 1), y_count)
        src, dst = ag.at[c, core, at], ag.at[c, core, at]
        if ref is not None:
            src = ref
        if hop + 1 == far:
            src, dst = src.at[pl.ds(*halves[way])], dst.at[pl.ds(*halves[way])]
        return remote(src, dst, ring_send.at[c, way, hop], ring_recv.at[c, way, hop], {"seq": neighbours[way]})

    def ring_wait(c, way, hop):
        at = lax.rem(y + (hop + 1) * (y_count - 1 if way == 0 else 1), y_count)
        ref = ag.at[c, core, at]
        if hop + 1 == far:
            ref = ref.at[pl.ds(*halves[way])]
        wait_bytes(ref, ring_recv.at[c, way, hop])
        return ref

    def to_sibling(c, src, dst):
        remote(src, dst, sib_send.at[c], sib_recv.at[c], {"seq": sibling}).start()

    for c in range(CHUNKS):
        for way in range(2):
            ring_copy(c, way, 0, att.at[c]).start()
        to_sibling(c, att.at[c], ag.at[c, core, y])
        pltpu.make_async_copy(att.at[c], ag.at[c, core, y], own_sem.at[c]).start()
    for c in range(CHUNKS):
        lanes = pl.ds(pl.multiple_of(core * HALF + c * CH, HEAD_DIM), CH)
        mine = rows_out.at[:, y, :, lanes]

        def send(d, c=c, mine=mine):
            other = lax.rem(seq + d, seq_count)
            remote(ret.at[c, :, other], mine, ret_send.at[c], ret_recv, {"seq": other}).start()

        pltpu.make_async_copy(ret.at[c, :, seq], mine, ret_recv).start()
        loop(1, seq_count, send)

    def weigh(c):
        for kc in range(CORES):
            def pair(i):
                left = jnp.concatenate([grad[2 * i], grad[2 * i + 1]], axis=1)
                right = jnp.concatenate([ag[c, kc, :, 2 * i + j].reshape(patches, CH) for j in range(2)], axis=0)
                turn[pl.ds(0, width)] += dot(left, right, ((1,), (0,)))

            turn[...] = jnp.zeros_like(turn)
            loop(0, frames // 2, pair)
            terms = jnp.sum(ag[c, kc, :, frames].astype(jnp.float32), axis=0)
            row = lax.broadcasted_iota(jnp.int32, (POS, CH), 0)
            packed = hi_lo(terms[0:1] + terms[1:2], row, 0) + hi_lo(terms[2:3] + terms[3:4], row, 2)
            turn[pl.ds(width, POS)] = packed
            zsend[c, :, kc] = turn[...].T.astype(jnp.bfloat16).reshape(z_count, share, LANES)
        if z_count > 1:
            def give(d):
                other = lax.rem(z + d, z_count)
                remote(
                    zsend.at[c, other], zrecv.at[c, z], z_send.at[c], z_recv.at[c], {"grp": x * z_count + other}
                ).start()

            loop(1, z_count, give)
        zrecv[c, z] = zsend[c, z]

    def project(c):
        def frame(f):
            total = jnp.zeros((width, patches), jnp.float32)
            for kc in range(CORES):
                lanes = slice(kc * HALF + c * CH, kc * HALF + (c + 1) * CH)
                total = total + dot(weight[:, lanes], ag[c, kc, :, f].reshape(patches, CH), ((1,), (1,)))
            if c > 0:
                total = total + acc[f]
            if c + 1 < CHUNKS:
                acc[f] = total
            else:
                proj_out[f] = total.astype(jnp.bfloat16)

        loop(0, frames, frame)

    for c in range(CHUNKS):
        for hop in range(far):
            for way in range(2):
                ref = ring_wait(c, way, hop)
                if hop + 1 < far:
                    ring_copy(c, way, hop + 1).start()
                to_sibling(c, ref, ref)
        wait_bytes(ag.at[c, core, y], own_sem.at[c])
        wait_bytes(ag.at[c, 1 - core], sib_recv.at[c])
        for kc in range(CORES):
            lanes = pl.ds(kc * HALF + c * CH, CH)
            pltpu.make_async_copy(ag.at[c, kc, :, seq], att_out.at[:, :, lanes], att_sem).start()
        weigh(c)
        project(c)
    for c in range(CHUNKS):
        if z_count > 1:
            wait_bytes(zrecv.at[c, pl.ds(0, z_count - 1)], z_recv.at[c])
        sums = jnp.sum(zrecv[c].astype(jnp.float32), axis=0)
        for kc in range(CORES):
            xsend[kc * CHUNKS + c] = sums[kc]

    def last(d):
        other = lax.rem(x + d, X)
        remote(xsend.at[other], xrecv.at[x], x_send, x_recv, {"grp": other * z_count + z}).start()

    loop(1, X, last)
    xrecv[x] = xsend[x]
    wait_bytes(att_out, att_sem)
    wait_bytes(rows_out, ret_recv)
    wait_bytes(xrecv.at[pl.ds(0, X - 1)], x_recv)
    token_root = float(frames * patches * z_count * X) ** 0.5
    wide_out[...] = jnp.sum(xrecv[...], axis=0) / token_root
    wait_bytes(xsend.at[pl.ds(0, X - 1)], x_send)
    for c in range(CHUNKS):
        if z_count > 1:
            wait_bytes(zsend.at[c, pl.ds(0, z_count - 1)], z_send.at[c])
        wait_bytes(ret.at[c, :, pl.ds(0, seq_count - 1)], ret_send.at[c])
        wait_bytes(ag.at[c, core], sib_send.at[c])
        for way in range(2):
            for hop in range(far):
                ring_copy(c, way, hop).wait_send()


def body(
    query_rows,
    key_rows,
    value_rows,
    out_grad,
    proj_grad,
    proj_weight,
    query_gain,
    key_gain,
    clip_of_frame,
    patch_count,
):
    bf16, f32 = jnp.bfloat16, jnp.float32
    patches, channels = query_rows.shape[1:]
    seq_count, group_count = lax.axis_size("seq"), lax.axis_size("grp")
    y_count, z_count = seq_count // CORES, group_count // X
    frames = seq_count
    width = proj_weight.shape[0]
    share = channels // group_count
    rows = frames * POS
    wide = BLOCK_POS * frames
    group_index, seq_index = lax.axis_index("grp"), lax.axis_index("seq")
    vmem, anywhere = pl.BlockSpec(memory_space=pltpu.VMEM), pl.BlockSpec(memory_space=pl.ANY)
    dma = pltpu.SemaphoreType.DMA

    placed = jnp.zeros((8, channels), f32)
    placed = lax.dynamic_update_slice(placed, jnp.stack((query_gain, key_gain)), (0, group_index * share))
    placed = lax.dynamic_slice_in_dim(placed, lax.rem(seq_index, CORES) * HALF, HALF, 1)

    win, gains = pl.pallas_call(
        exchange_kernel,
        out_shape=(
            jax.ShapeDtypeStruct((CHUNKS, 3, 4, frames, POS, CH), bf16),
            jax.ShapeDtypeStruct((8, HALF), f32),
        ),
        in_specs=[anywhere] * 4 + [vmem],
        out_specs=(anywhere, vmem),
        scratch_shapes=[
            pltpu.VMEM((4, y_count, POS, channels), bf16),
            pltpu.VMEM((z_count, 8, HALF), f32),
            pltpu.VMEM((X, 8, HALF), f32),
            pltpu.VMEM((8, HALF), f32),
            dma((4,)),
            dma((CHUNKS,)),
            dma((CHUNKS,)),
            dma((CHUNKS, 2)),
            dma((CHUNKS, 2)),
            dma((2,)),
            dma((2,)),
        ],
        compiler_params=pltpu.CompilerParams(collective_id=0, has_side_effects=True, vmem_limit_bytes=VMEM_LIMIT),
        name="exchange",
    )(*(a.reshape(y_count, POS, channels) for a in (query_rows, key_rows, value_rows, out_grad)), placed)

    border = jnp.full((frames,), -1, jnp.int32)
    clip_padded = jnp.concatenate([border, clip_of_frame, border])
    nearby = lax.dynamic_slice_in_dim(clip_padded, group_index * frames, 3 * frames, 0).reshape(3, frames)
    nearby = jnp.stack((nearby[1], nearby[0], nearby[2]))
    slots = jnp.arange(patch_count.shape[0], dtype=jnp.int32)
    counts = jnp.sum(jnp.where(nearby[..., None] == slots, patch_count, 0), axis=-1)
    offset = jnp.arange(BLOCK_POS, dtype=jnp.int32)[None, :, None]
    codes = (nearby[:, None, :] * BLOCK_POS + offset).reshape(3 * wide)
    limit = (counts[:, None, :] - offset).reshape(3 * wide, 1)
    index = jnp.arange(rows, dtype=jnp.int32)
    source = index % frames * POS + index // frames
    perm = (source[:, None] == index[None, :]).astype(bf16)

    whole = lambda shape: pl.BlockSpec(shape, lambda c: (0,) * len(shape))
    ret, att = pl.pallas_call(
        attend_kernel,
        grid=(CHUNKS,),
        out_shape=(
            jax.ShapeDtypeStruct((CHUNKS, 3, frames, POS, CH), bf16),
            jax.ShapeDtypeStruct((CHUNKS, frames + 1, POS, CH), bf16),
        ),
        in_specs=[
            pl.BlockSpec((1, 3, 4, frames, POS, CH), lambda c: (c, 0, 0, 0, 0, 0)),
            pl.BlockSpec((8, CH), lambda c: (0, c)),
            whole((3 * wide, 1)),
            whole((1, 3 * wide)),
            whole((3 * wide, 1)),
            whole((rows, rows)),
            whole((rows, rows)),
        ],
        out_specs=(
            pl.BlockSpec((1, 3, frames, POS, CH), lambda c: (c, 0, 0, 0, 0)),
            pl.BlockSpec((1, frames + 1, POS, CH), lambda c: (c, 0, 0, 0)),
        ),
        scratch_shapes=[
            pltpu.VMEM((4, CHUNK_HEADS, 3, rows, HEAD_DIM), bf16),
            pltpu.VMEM((2, CHUNK_HEADS, rows, HEAD_DIM), f32),
            pltpu.VMEM((3 * wide, 3 * wide), f32),
            pltpu.VMEM((4, rows, CH), bf16),
        ],
        compiler_params=pltpu.CompilerParams(vmem_limit_bytes=VMEM_LIMIT),
        name="attend",
    )(win, gains, codes[:, None], codes[None, :], limit, perm, perm.T)

    far = y_count // 2
    rows_out, att_out, projected, wide_out = pl.pallas_call(
        collect_kernel,
        out_shape=(
            jax.ShapeDtypeStruct((3, y_count, POS, channels), bf16),
            jax.ShapeDtypeStruct((y_count, POS, channels), bf16),
            jax.ShapeDtypeStruct((frames, width, patches), bf16),
            jax.ShapeDtypeStruct((share, LANES), f32),
        ),
        in_specs=[anywhere, anywhere, vmem, vmem],
        out_specs=(anywhere, anywhere, vmem, vmem),
        scratch_shapes=[
            pltpu.VMEM((CHUNKS, CORES, y_count, frames + 1, POS, CH), bf16),
            pltpu.VMEM((frames, width, patches), f32),
            pltpu.VMEM((LANES, CH), f32),
            pltpu.VMEM((CHUNKS, z_count, CORES, share, LANES), bf16),
            pltpu.VMEM((CHUNKS, z_count, CORES, share, LANES), bf16),
            pltpu.VMEM((X, share, LANES), f32),
            pltpu.VMEM((X, share, LANES), f32),
            dma((CHUNKS,)),
            dma,
            dma((CHUNKS,)),
            dma((CHUNKS, 2, far)),
            dma((CHUNKS, 2, far)),
            dma((CHUNKS,)),
            dma((CHUNKS,)),
            dma((CHUNKS,)),
            dma((CHUNKS,)),
            dma,
            dma,
            dma,
        ],
        compiler_params=pltpu.CompilerParams(collective_id=1, has_side_effects=True, vmem_limit_bytes=VMEM_LIMIT),
        name="collect",
    )(ret, att, proj_grad, proj_weight)

    shape = (1, patches, channels)
    return (
        att_out.reshape(shape),
        projected,
        rows_out[0].reshape(shape),
        rows_out[1].reshape(shape),
        rows_out[2].reshape(shape),
        wide_out[:, :width],
        wide_out[:, width] + wide_out[:, width + 1],
        wide_out[:, width + 2] + wide_out[:, width + 3],
    )


def solution(mesh):
    rows = P(("grp", "seq"), None, None)
    in_specs = (rows, rows, rows, rows, P("grp", "seq", None), P("seq", None), P("grp"), P("grp"), P(), P())
    out_specs = (rows, P("grp", "seq", None), rows, rows, rows, P("grp", "seq"), P("grp"), P("grp"))
    return jax.shard_map(body, mesh=mesh, in_specs=in_specs, out_specs=out_specs, check_vma=False)
```

```python
import jax
import jax.numpy as jnp
from jax import lax
from jax.experimental import pallas as pl
from jax.experimental.pallas import tpu as pltpu
from jax.sharding import PartitionSpec as P

HEADS = 12
HEAD_DIM = 128
EPS = 1e-06
NEGATIVE = -1e30
SCALE = HEAD_DIM ** (-0.5)
MESH = pl.DeviceIdType.MESH

POS = 16
CORES = 2
CHUNKS = 3
CHUNK_HEADS = HEADS // (CORES * CHUNKS)
CH = CHUNK_HEADS * HEAD_DIM
HALF = CHUNKS * CH
X = 4
BLOCK_POS = 8
LANES = 256
VMEM_LIMIT = 60 * 1024 * 1024


def dot(a, b, dims):
    return lax.dot_general(a, b, (dims, ((), ())), preferred_element_type=jnp.float32)


def place():
    seq_count = lax.axis_size("seq")
    group_count = lax.axis_size("grp")
    grp, seq = lax.axis_index("grp"), lax.axis_index("seq")
    z_count, y_count = group_count // X, seq_count // CORES
    return (
        grp, seq, z_count, y_count,
        lax.div(grp, z_count), lax.rem(grp, z_count),
        lax.div(seq, CORES), lax.rem(seq, CORES),
    )


def wait_bytes(ref, sem):
    pltpu.make_async_copy(ref, ref, sem).wait()


def remote(src, dst, send_sem, recv_sem, device):
    return pltpu.make_async_remote_copy(
        src_ref=src, dst_ref=dst, send_sem=send_sem, recv_sem=recv_sem, device_id=device, device_id_type=MESH
    )


def loop(low, high, step):
    def one(i, carry):
        step(i)
        return carry

    lax.fori_loop(low, high, one, 0)


def greet():
    grp, seq, z_count, y_count, x, z, y, core = place()
    seq_count, group_count = y_count * CORES, z_count * X
    barrier = pltpu.get_barrier_semaphore()

    def signal(device):
        pl.semaphore_signal(barrier, inc=1, device_id=device, device_id_type=MESH)

    loop(1, seq_count, lambda d: signal({"seq": lax.rem(seq + d, seq_count)}))
    if z_count > 1:
        loop(1, z_count, lambda d: signal({"grp": x * z_count + lax.rem(z + d, z_count)}))
    loop(1, X, lambda d: signal({"grp": lax.rem(x + d, X) * z_count + z}))
    for step in (1, group_count - 1):
        signal({"grp": lax.rem(grp + step, group_count)})
    pl.semaphore_wait(barrier, seq_count + z_count + X - 1)


def mean_lanes(values):
    return jnp.mean(values, axis=-1, keepdims=True)


def hi_lo(total, row, first):
    high = total.astype(jnp.bfloat16).astype(jnp.float32)
    low = total - high
    return jnp.where(row == first, high, 0.0) + jnp.where(row == first + 1, low, 0.0)


def iota(shape, dim):
    return lax.broadcasted_iota(jnp.int32, shape, dim)


def fused_kernel(
    q, k, v, g, query_gain, key_gain, clip, count, grad, weight,
    rows_out, proj_out, wide_out, gain_out,
    stage, win, normed, held, bias, limit, perms, back, ret, att, ag, tokens, w, turn, zall, zrecv, xsend, xrecv, gz, gx, gs, gains,
    load_sem, send_sem, recv_sem, halo_send, halo_recv, gain_send, gain_recv,
    ret_send, ret_recv, own_sem, ring_send, ring_recv, sib_send, sib_recv, z_send, z_recv, x_send, x_recv,
):
    grp, seq, z_count, y_count, x, z, y, core = place()
    seq_count, group_count = y_count * CORES, z_count * X
    frames, width, patches = grad.shape
    rows = frames * POS
    wide = BLOCK_POS * frames
    share = HALF * CORES // group_count
    far = y_count // 2
    f32, bf16 = jnp.float32, jnp.bfloat16

    loads = [pltpu.make_async_copy(ref, stage.at[i], load_sem.at[i]) for i, ref in enumerate((q, k, v, g))]
    for load in loads:
        load.start()
    for f in range(frames):
        pltpu.make_async_copy(grad.at[f], tokens.at[:, pl.ds(f * patches, patches)], load_sem.at[4]).start()
    pltpu.make_async_copy(weight, w, load_sem.at[5]).start()

    lane, sub = iota((8, HALF), 1), iota((8, HALF), 0)
    gs[...] = jnp.zeros_like(gs)

    def put_gain(i):
        at = lane == grp * share + i - core * HALF
        gs[...] += jnp.where(at & (sub == 0), query_gain[i], 0.0) + jnp.where(at & (sub == 1), key_gain[i], 0.0)

    loop(0, share, put_gain)
    greet()

    if z_count > 1:
        loop(
            1, z_count,
            lambda d: remote(
                gs, gz.at[z], gain_send.at[0], gain_recv.at[0], {"grp": x * z_count + lax.rem(z + d, z_count)}
            ).start(),
        )
    for load in loads:
        load.wait()
    for c in range(CHUNKS):
        def spread_out(i, c=c):
            odd = lax.rem(i, 2)
            dy = odd * lax.div(i + 1, 2) + (1 - odd) * (y_count - lax.div(i, 2))
            other = lax.rem(y + dy, y_count)
            for cc in range(CORES):
                remote(
                    stage.at[:, other, :, pl.ds(cc * HALF + c * CH, CH)], win.at[c, 0, :, seq],
                    send_sem.at[c], recv_sem.at[c], {"seq": other * CORES + cc},
                ).start()

        loop(1, y_count, spread_out)
        remote(
            stage.at[:, y, :, pl.ds(pl.multiple_of((1 - core) * HALF + c * CH, HEAD_DIM), CH)],
            win.at[c, 0, :, seq], send_sem.at[c], recv_sem.at[c], {"seq": y * CORES + 1 - core},
        ).start()
        pltpu.make_async_copy(
            stage.at[:, y, :, pl.ds(pl.multiple_of(core * HALF + c * CH, HEAD_DIM), CH)],
            win.at[c, 0, :, seq], recv_sem.at[c],
        ).start()

    def code_of(index, slot):
        at = (grp + (0, -1, 1)[slot]) * frames + index
        inside = (at >= 0) & (at < frames * group_count)
        own_clip = clip[lax.rem(at + frames * group_count, frames * group_count)]
        return jnp.where(inside, own_clip, -1), jnp.where(inside, count[own_clip], 0)

    col, row = iota((3 * wide, 1), 0), iota((1, 3 * wide), 1)
    col_code, row_code = jnp.zeros((3 * wide, 1), jnp.int32), jnp.zeros((1, 3 * wide), jnp.int32)
    col_count = jnp.zeros((3 * wide, 1), jnp.int32)
    for slot in range(3):
        def put_code(i, carry, slot=slot):
            col_code, row_code, col_count = carry
            code, most = code_of(i, slot)

            def here(index):
                return (lax.div(index, wide) == slot) & (lax.rem(index, frames) == i)

            return (
                jnp.where(here(col), code, col_code),
                jnp.where(here(row), code, row_code),
                jnp.where(here(col), most, col_count),
            )

        col_code, row_code, col_count = lax.fori_loop(0, frames, put_code, (col_code, row_code, col_count))

    def position(index):
        return lax.div(lax.rem(index, wide), frames)

    bias[...] = jnp.where((col_code == row_code) & (position(col) == position(row)), 0.0, NEGATIVE)
    limit[...] = col_count - position(col)
    down, across = iota((rows, rows), 0), iota((rows, rows), 1)
    for i, (one, other) in enumerate(((down, across), (across, down))):
        source = lax.rem(one, frames) * POS + lax.div(one, frames)
        perms[i] = jnp.where(source == other, 1.0, 0.0).astype(bf16)

    gz[z] = gs[...]
    if z_count > 1:
        wait_bytes(gz.at[pl.ds(0, z_count - 1)], gain_recv.at[0])
        wait_bytes(gz.at[pl.ds(0, z_count - 1)], gain_send.at[0])
    gs[...] = jnp.sum(gz[...], axis=0)
    loop(
        1, X,
        lambda d: remote(
            gs, gx.at[x], gain_send.at[1], gain_recv.at[1], {"grp": lax.rem(x + d, X) * z_count + z}
        ).start(),
    )
    gx[x] = gs[...]

    def halo(c, way):
        return remote(
            win.at[c, 0], win.at[c, 1 + way], halo_send.at[c, way], halo_recv.at[c, way],
            {"grp": lax.rem(grp + (1, group_count - 1)[way], group_count)},
        )

    def to_neighbours(c):
        wait_bytes(win.at[c, 0], recv_sem.at[c])
        for way in range(2):
            halo(c, way).start()

    def attend(c, between):
        lanes_of = [slice(h * HEAD_DIM, (h + 1) * HEAD_DIM) for h in range(CHUNK_HEADS)]
        gain_of = [
            [gains[a : a + 1, c * CH + h * HEAD_DIM : c * CH + (h + 1) * HEAD_DIM] for a in range(2)]
            for h in range(CHUNK_HEADS)
        ]

        def gather(slot):
            for a in range(4):
                moved = dot(perms[0], win[c, slot, a].reshape(rows, CH), ((1,), (0,)))
                for h in range(CHUNK_HEADS):
                    part = moved[:, lanes_of[h]]
                    if a < 2:
                        inverse = lax.rsqrt(mean_lanes(part * part) + EPS)
                        normed[a, h, slot] = (part * inverse * gain_of[h][a]).astype(bf16)

                        @pl.when(slot == 0)
                        def _():
                            held[a, h] = part
                    else:
                        normed[a, h, slot] = part.astype(bf16)

        loop(0, 3, gather)
        between[0]()

        def block(b, sums):
            at = pl.ds(pl.multiple_of(b * wide, wide), wide)
            live = jnp.where(limit[...] > y * POS + b * BLOCK_POS, 1.0, 0.0)
            new = []
            for h in range(CHUNK_HEADS):
                query, key, value, cotangent = (
                    normed[a, h, :, at, :].reshape(3 * wide, HEAD_DIM) for a in range(4)
                )
                scores = dot(query, key, ((1,), (1,))) * SCALE + bias[...]
                prob_grad = dot(cotangent, value, ((1,), (1,)))
                spread = jnp.exp(scores - jnp.max(scores, axis=-1, keepdims=True))
                probs = spread * (live / jnp.sum(spread, axis=-1, keepdims=True))
                rounded = probs.astype(bf16)
                attended = dot(rounded, value, ((1,), (0,))).astype(bf16)
                delta = jnp.sum(cotangent.astype(f32) * attended.astype(f32), axis=-1, keepdims=True)
                score_grad = (probs * (prob_grad - delta) * SCALE).astype(bf16)
                back[0, at, lanes_of[h]] = attended[:wide]
                back[3, at, lanes_of[h]] = dot(rounded[:, :wide], cotangent, ((0,), (0,))).astype(bf16)
                ups = (
                    dot(score_grad[:wide], key, ((1,), (0,))),
                    dot(score_grad[:, :wide], query, ((0,), (0,))),
                )
                for a in range(2):
                    up = ups[a].astype(bf16).astype(f32)
                    rows_in = held[a, h, at, :]
                    inverse = lax.rsqrt(mean_lanes(rows_in * rows_in) + EPS)
                    weighted = up * gain_of[h][a]
                    along = mean_lanes(weighted * rows_in)
                    scaled = rows_in * inverse
                    back[1 + a, at, lanes_of[h]] = (
                        inverse * weighted - scaled * inverse * inverse * along
                    ).astype(bf16)
                    new.append(sums[len(new)] + jnp.sum(up * scaled, axis=0, keepdims=True))
            return tuple(new)

        zero = jnp.zeros((1, HEAD_DIM), f32)
        sums = lax.fori_loop(0, POS // BLOCK_POS, block, (zero,) * (2 * CHUNK_HEADS))
        between[1]()
        for a in range(4):
            out = dot(perms[1], back[a], ((1,), (0,))).astype(bf16).reshape(frames, POS, CH)
            if a == 0:
                att[c, pl.ds(0, frames)] = out
            else:
                ret[c, a - 1] = out
        at_row = iota((POS, CH), 0)
        packed = jnp.zeros((POS, CH), f32)
        for a in range(2):
            packed = packed + hi_lo(jnp.concatenate(sums[a::2], axis=1), at_row, 2 * a)
        att[c, frames] = packed.astype(bf16)

    neighbours = (lax.rem(y + 1, y_count) * CORES + core, lax.rem(y + y_count - 1, y_count) * CORES + core)
    sibling = y * CORES + 1 - core
    first_part = (frames + 1) // 2
    halves = ((0, first_part), (first_part, frames + 1 - first_part))

    def ring_copy(c, way, hop, ref=None):
        at = lax.rem(y + hop * (y_count - 1 if way == 0 else 1), y_count)
        src, dst = ag.at[c, core, at], ag.at[c, core, at]
        if ref is not None:
            src = ref
        if hop + 1 == far:
            src, dst = src.at[pl.ds(*halves[way])], dst.at[pl.ds(*halves[way])]
        return remote(src, dst, ring_send.at[c, way, hop], ring_recv.at[c, way, hop], {"seq": neighbours[way]})

    def to_sibling(c, src, dst):
        remote(src, dst, sib_send.at[c], sib_recv.at[c], {"seq": sibling}).start()

    def ring_step(c, hop):
        for way in range(2):
            at = lax.rem(y + (hop + 1) * (y_count - 1 if way == 0 else 1), y_count)
            ref = ag.at[c, core, at]
            if hop + 1 == far:
                ref = ref.at[pl.ds(*halves[way])]
            wait_bytes(ref, ring_recv.at[c, way, hop])
            if hop + 1 < far:
                ring_copy(c, way, hop + 1).start()
            to_sibling(c, ref, ref)

    def give_back(c):
        for way in range(2):
            ring_copy(c, way, 0, att.at[c]).start()
        to_sibling(c, att.at[c], ag.at[c, core, y])
        pltpu.make_async_copy(att.at[c], ag.at[c, core, y], own_sem.at[c]).start()
        mine = rows_out.at[pl.ds(0, 3), y, :, pl.ds(pl.multiple_of(core * HALF + c * CH, HEAD_DIM), CH)]

        def send(d):
            other = lax.rem(seq + d, seq_count)
            remote(ret.at[c, :, other], mine, ret_send.at[c], ret_recv, {"seq": other}).start()

        pltpu.make_async_copy(ret.at[c, :, seq], mine, ret_recv).start()
        loop(1, seq_count, send)

    units = 2 * z_count
    turn[...] = jnp.zeros_like(turn)

    def weigh(c):
        wait_bytes(ag.at[c, core, y], own_sem.at[c])
        wait_bytes(ag.at[c, 1 - core], sib_recv.at[c])
        for kc in range(CORES):
            pltpu.make_async_copy(
                ag.at[c, kc, :, seq], rows_out.at[3, :, :, pl.ds(kc * HALF + c * CH, CH)], ret_recv
            ).start()
            right = jnp.concatenate([ag[c, kc, :, f].reshape(patches, CH) for f in range(frames)], axis=0)
            turn[pl.ds(0, width)] = dot(tokens[...], right, ((1,), (0,)))
            terms = jnp.sum(ag[c, kc, :, frames].astype(f32), axis=0)
            at_row = iota((POS, CH), 0)
            packed = hi_lo(terms[0:1] + terms[1:2], at_row, 0) + hi_lo(terms[2:3] + terms[3:4], at_row, 2)
            turn[pl.ds(width, POS)] = packed
            zall[kc, pl.ds(c * CH, CH)] = turn[...].T.astype(bf16)
        if z_count > 1:
            for unit in range(units * c // CHUNKS, units * (c + 1) // CHUNKS):
                pair, owner = unit // z_count, unit % z_count

                @pl.when(z != owner)
                def _(unit=unit, pair=pair, owner=owner):
                    remote(
                        zall.at[:, pl.ds(unit * share, share)], zrecv.at[pair, z], z_send.at[pair], z_recv.at[pair],
                        {"grp": x * z_count + owner},
                    ).start()

    def project():
        def frame_pair(i):
            left = jnp.concatenate(
                [
                    jnp.concatenate(
                        [ag[c, kc, :, 2 * i + j].reshape(patches, CH) for kc in range(CORES) for c in range(CHUNKS)], axis=1
                    )
                    for j in range(2)
                ],
                axis=0,
            )
            total = dot(w[...], left, ((1,), (1,))).astype(bf16)
            for j in range(2):
                proj_out[2 * i + j] = total[:, j * patches : (j + 1) * patches]

        loop(0, frames // 2, frame_pair)

    def steps(*which):
        def run():
            for c, hop in which:
                if hop < far:
                    ring_step(c, hop)

        return run

    to_neighbours(0)
    wait_bytes(gx.at[pl.ds(0, X - 1)], gain_recv.at[1])
    gains[...] = jnp.sum(gx[...], axis=0)
    to_neighbours(1)
    for way in range(2):
        halo(0, way).wait_recv()
    attend(0, (steps(), steps()))
    give_back(0)
    to_neighbours(2)
    for way in range(2):
        halo(1, way).wait_recv()
    attend(1, (steps((0, 0)), steps((0, 1))))
    give_back(1)
    for way in range(2):
        halo(2, way).wait_recv()
    attend(2, (steps((0, 2), (1, 0)), steps((0, 3), (1, 1))))
    give_back(2)
    for load in (pltpu.make_async_copy(tokens, tokens, load_sem.at[4]), pltpu.make_async_copy(weight, w, load_sem.at[5])):
        load.wait()
    steps((1, 2), (2, 0))()
    weigh(0)
    steps((1, 3), (2, 1))()
    weigh(1)
    steps((2, 2), (2, 3))()
    weigh(2)
    project()
    for pair in range(2):
        if z_count > 1:
            wait_bytes(zrecv.at[pair, pl.ds(0, z_count - 1)], z_recv.at[pair])
        own = zall[:, pl.ds(pl.multiple_of((pair * z_count + z) * share, POS), share)]
        zrecv[pair, z] = own
        sums = jnp.sum(zrecv[pair].astype(f32), axis=0)
        for kc in range(CORES):
            xsend[2 * kc + pair] = sums[kc]

    def last(d):
        other = lax.rem(x + d, X)
        remote(xsend.at[other], xrecv.at[x], x_send, x_recv, {"grp": other * z_count + z}).start()

    loop(1, X, last)
    xrecv[x] = xsend[x]
    for c in range(CHUNKS):
        wait_bytes(win.at[c, 0, :, pl.ds(0, seq_count - 1)], send_sem.at[c])
        wait_bytes(ret.at[c, :, pl.ds(0, seq_count - 1)], ret_send.at[c])
        wait_bytes(ag.at[c, core], sib_send.at[c])
        for way in range(2):
            halo(c, way).wait_send()
            for hop in range(far):
                ring_copy(c, way, hop).wait_send()
    if z_count > 1:
        for pair in range(2):
            wait_bytes(zrecv.at[pair, pl.ds(0, z_count - 1)], z_send.at[pair])
    wait_bytes(gx.at[pl.ds(0, X - 1)], gain_send.at[1])
    wait_bytes(rows_out, ret_recv)
    wait_bytes(xrecv.at[pl.ds(0, X - 1)], x_recv)
    token_root = float(frames * patches * group_count) ** 0.5
    total = jnp.sum(xrecv[...], axis=0) / token_root
    wide_out[...] = total[:, :width]
    terms = total.T
    gain_out[0:1] = terms[width : width + 1] + terms[width + 1 : width + 2]
    gain_out[1:2] = terms[width + 2 : width + 3] + terms[width + 3 : width + 4]
    wait_bytes(xsend.at[pl.ds(0, X - 1)], x_send)


def body(
    query_rows,
    key_rows,
    value_rows,
    out_grad,
    proj_grad,
    proj_weight,
    query_gain,
    key_gain,
    clip_of_frame,
    patch_count,
):
    bf16, f32 = jnp.bfloat16, jnp.float32
    patches, channels = query_rows.shape[1:]
    seq_count, group_count = lax.axis_size("seq"), lax.axis_size("grp")
    y_count, z_count = seq_count // CORES, group_count // X
    frames = seq_count
    width = proj_weight.shape[0]
    share = channels // group_count
    rows = frames * POS
    wide = BLOCK_POS * frames
    far = y_count // 2
    vmem, smem = pl.BlockSpec(memory_space=pltpu.VMEM), pl.BlockSpec(memory_space=pltpu.SMEM)
    anywhere = pl.BlockSpec(memory_space=pl.ANY)
    dma = pltpu.SemaphoreType.DMA
    rows_out, projected, wide_out, gain_out = pl.pallas_call(
        fused_kernel,
        out_shape=(
            jax.ShapeDtypeStruct((4, y_count, POS, channels), bf16),
            jax.ShapeDtypeStruct((frames, width, patches), bf16),
            jax.ShapeDtypeStruct((share, width), f32),
            jax.ShapeDtypeStruct((2, share), f32),
        ),
        in_specs=[anywhere] * 4 + [smem] * 4 + [anywhere] * 2,
        out_specs=(anywhere, vmem, vmem, vmem),
        scratch_shapes=[
            pltpu.VMEM((4, y_count, POS, channels), bf16),
            pltpu.VMEM((CHUNKS, 3, 4, frames, POS, CH), bf16),
            pltpu.VMEM((4, CHUNK_HEADS, 3, rows, HEAD_DIM), bf16),
            pltpu.VMEM((2, CHUNK_HEADS, rows, HEAD_DIM), f32),
            pltpu.VMEM((3 * wide, 3 * wide), f32),
            pltpu.VMEM((3 * wide, 1), jnp.int32),
            pltpu.VMEM((2, rows, rows), bf16),
            pltpu.VMEM((4, rows, CH), bf16),
            pltpu.VMEM((CHUNKS, 3, frames, POS, CH), bf16),
            pltpu.VMEM((CHUNKS, frames + 1, POS, CH), bf16),
            pltpu.VMEM((CHUNKS, CORES, y_count, frames + 1, POS, CH), bf16),
            pltpu.VMEM((width, frames * patches), bf16),
            pltpu.VMEM((width, channels), bf16),
            pltpu.VMEM((LANES, CH), f32),
            pltpu.VMEM((CORES, HALF, LANES), bf16),
            pltpu.VMEM((2, z_count, CORES, share, LANES), bf16),
            pltpu.VMEM((X, share, LANES), f32),
            pltpu.VMEM((X, share, LANES), f32),
            pltpu.VMEM((z_count, 8, HALF), f32),
            pltpu.VMEM((X, 8, HALF), f32),
            pltpu.VMEM((8, HALF), f32),
            pltpu.VMEM((8, HALF), f32),
            dma((6,)),
            dma((CHUNKS,)),
            dma((CHUNKS,)),
            dma((CHUNKS, 2)),
            dma((CHUNKS, 2)),
            dma((2,)),
            dma((2,)),
            dma((CHUNKS,)),
            dma,
            dma((CHUNKS,)),
            dma((CHUNKS, 2, far)),
            dma((CHUNKS, 2, far)),
            dma((CHUNKS,)),
            dma((CHUNKS,)),
            dma((2,)),
            dma((2,)),
            dma,
            dma,
        ],
        compiler_params=pltpu.CompilerParams(collective_id=0, has_side_effects=True, vmem_limit_bytes=VMEM_LIMIT),
        name="fused",
    )(
        *(a.reshape(y_count, POS, channels) for a in (query_rows, key_rows, value_rows, out_grad)),
        query_gain, key_gain, clip_of_frame, patch_count, proj_grad, proj_weight,
    )
    shape = (1, patches, channels)
    return (
        rows_out[3].reshape(shape),
        projected,
        rows_out[0].reshape(shape),
        rows_out[1].reshape(shape),
        rows_out[2].reshape(shape),
        wide_out,
        gain_out[0],
        gain_out[1],
    )


def solution(mesh):
    rows = P(("grp", "seq"), None, None)
    in_specs = (rows, rows, rows, rows, P("grp", "seq", None), P("seq", None), P("grp"), P("grp"), P(), P())
    out_specs = (rows, P("grp", "seq", None), rows, rows, rows, P("grp", "seq"), P("grp"), P("grp"))
    return jax.shard_map(body, mesh=mesh, in_specs=in_specs, out_specs=out_specs, check_vma=False)
```

```python
import jax
import jax.numpy as jnp
from jax import lax
from jax.experimental import pallas as pl
from jax.experimental.pallas import tpu as pltpu
from jax.sharding import PartitionSpec as P

HEADS = 12
HEAD_DIM = 128
EPS = 1e-06
NEGATIVE = -1e30
SCALE = HEAD_DIM ** (-0.5)
MESH = pl.DeviceIdType.MESH

POS = 16
CORES = 2
CHUNKS = 3
CHUNK_HEADS = HEADS // (CORES * CHUNKS)
CH = CHUNK_HEADS * HEAD_DIM
HALF = CHUNKS * CH
X = 4
BLOCK_POS = 8
LANES = 256
VMEM_LIMIT = 28 * 1024 * 1024


def dot(a, b, dims):
    return lax.dot_general(a, b, (dims, ((), ())), preferred_element_type=jnp.float32)


def place():
    seq_count = lax.axis_size("seq")
    group_count = lax.axis_size("grp")
    grp, seq = lax.axis_index("grp"), lax.axis_index("seq")
    z_count, y_count = group_count // X, seq_count // CORES
    return (
        grp, seq, z_count, y_count,
        lax.div(grp, z_count), lax.rem(grp, z_count),
        lax.div(seq, CORES), lax.rem(seq, CORES),
    )


def wait_bytes(ref, sem):
    pltpu.make_async_copy(ref, ref, sem).wait()


def remote(src, dst, send_sem, recv_sem, device):
    return pltpu.make_async_remote_copy(
        src_ref=src, dst_ref=dst, send_sem=send_sem, recv_sem=recv_sem, device_id=device, device_id_type=MESH
    )


def loop(low, high, step):
    def one(i, carry):
        step(i)
        return carry

    lax.fori_loop(low, high, one, 0)


def greet():
    grp, seq, z_count, y_count, x, z, y, core = place()
    seq_count, group_count = y_count * CORES, z_count * X
    barrier = pltpu.get_barrier_semaphore()

    def signal(device):
        pl.semaphore_signal(barrier, inc=1, device_id=device, device_id_type=MESH)

    loop(1, seq_count, lambda d: signal({"seq": lax.rem(seq + d, seq_count)}))
    loop(1, group_count, lambda d: signal({"grp": lax.rem(grp + d, group_count)}))
    return lambda: pl.semaphore_wait(barrier, seq_count + group_count - 2)


def mean_lanes(values):
    return jnp.mean(values, axis=-1, keepdims=True)


def hi_lo(total, row, first):
    high = total.astype(jnp.bfloat16).astype(jnp.float32)
    low = total - high
    return jnp.where(row == first, high, 0.0) + jnp.where(row == first + 1, low, 0.0)


def iota(shape, dim):
    return lax.broadcasted_iota(jnp.int32, shape, dim)


def fused_kernel(
    q, k, v, g, query_gain_in, key_gain_in, clip_in, count_in, grad, weight,
    rows_out, proj_out, wide_out, gain_out,
    stage, win, normed, held, bias, limit, perms, back, ret, att, ag, tokens, w, turn, zall, shares, gz, gx, gs, gains,
    query_gain, key_gain, clip, count,
    load_sem, send_sem, recv_sem, halo_send, halo_recv, gain_send, gain_recv,
    ret_send, ret_recv, own_sem, ring_send, ring_recv, sib_send, sib_recv, share_send, share_recv,
):
    grp, seq, z_count, y_count, x, z, y, core = place()
    seq_count, group_count = y_count * CORES, z_count * X
    frames, width, patches = grad.shape
    rows = frames * POS
    wide = BLOCK_POS * frames
    share = HALF * CORES // group_count
    far = y_count // 2
    f32, bf16 = jnp.float32, jnp.bfloat16

    loads = [pltpu.make_async_copy(ref, stage.at[i], load_sem.at[i]) for i, ref in enumerate((q, k, v, g))]
    for load in loads:
        load.start()
    for f in range(frames):
        pltpu.make_async_copy(grad.at[f], tokens.at[:, pl.ds(f * patches, patches)], load_sem.at[4]).start()
    pltpu.make_async_copy(weight, w, load_sem.at[5]).start()

    small = [
        pltpu.make_async_copy(ref, held_ref, load_sem.at[6 + i])
        for i, (ref, held_ref) in enumerate(
            ((query_gain_in, query_gain), (key_gain_in, key_gain), (clip_in, clip), (count_in, count))
        )
    ]
    for load in small:
        load.start()
    greeted = greet()

    greeted()

    for load in loads:
        load.wait()
    for c in range(CHUNKS):
        def spread_out(i, c=c):
            odd = lax.rem(i, 2)
            dy = odd * lax.div(i + 1, 2) + (1 - odd) * (y_count - lax.div(i, 2))
            other = lax.rem(y + dy, y_count)
            for cc in range(CORES):
                remote(
                    stage.at[:, other, :, pl.ds(cc * HALF + c * CH, CH)], win.at[c, 0, :, seq],
                    send_sem.at[c], recv_sem.at[c], {"seq": other * CORES + cc},
                ).start()

        loop(1, y_count, spread_out)
        remote(
            stage.at[:, y, :, pl.ds(pl.multiple_of((1 - core) * HALF + c * CH, HEAD_DIM), CH)],
            win.at[c, 0, :, seq], send_sem.at[c], recv_sem.at[c], {"seq": y * CORES + 1 - core},
        ).start()
        pltpu.make_async_copy(
            stage.at[:, y, :, pl.ds(pl.multiple_of(core * HALF + c * CH, HEAD_DIM), CH)],
            win.at[c, 0, :, seq], recv_sem.at[c],
        ).start()

    for load in small:
        load.wait()

    lane, sub = iota((8, HALF), 1), iota((8, HALF), 0)
    gs[...] = jnp.zeros_like(gs)

    def put_gain(i):
        at = lane == grp * share + i - core * HALF
        gs[...] += jnp.where(at & (sub == 0), query_gain[i], 0.0) + jnp.where(at & (sub == 1), key_gain[i], 0.0)

    loop(0, share, put_gain)
    if z_count > 1:
        loop(
            1, z_count,
            lambda d: remote(
                gs, gz.at[z], gain_send.at[0], gain_recv.at[0], {"grp": x * z_count + lax.rem(z + d, z_count)}
            ).start(),
        )
    def code_of(index, slot):
        at = (grp + (0, -1, 1)[slot]) * frames + index
        inside = (at >= 0) & (at < frames * group_count)
        own_clip = clip[lax.rem(at + frames * group_count, frames * group_count)]
        return jnp.where(inside, own_clip, -1), jnp.where(inside, count[own_clip], 0)

    col, row = iota((3 * wide, 1), 0), iota((1, 3 * wide), 1)
    col_code, row_code = jnp.zeros((3 * wide, 1), jnp.int32), jnp.zeros((1, 3 * wide), jnp.int32)
    col_count = jnp.zeros((3 * wide, 1), jnp.int32)
    for slot in range(3):
        def put_code(i, carry, slot=slot):
            col_code, row_code, col_count = carry
            code, most = code_of(i, slot)

            def here(index):
                return (lax.div(index, wide) == slot) & (lax.rem(index, frames) == i)

            return (
                jnp.where(here(col), code, col_code),
                jnp.where(here(row), code, row_code),
                jnp.where(here(col), most, col_count),
            )

        col_code, row_code, col_count = lax.fori_loop(0, frames, put_code, (col_code, row_code, col_count))

    def position(index):
        return lax.div(lax.rem(index, wide), frames)

    bias[...] = jnp.where((col_code == row_code) & (position(col) == position(row)), 0.0, NEGATIVE)
    limit[...] = col_count - position(col)
    down, across = iota((rows, rows), 0), iota((rows, rows), 1)
    for i, (one, other) in enumerate(((down, across), (across, down))):
        source = lax.rem(one, frames) * POS + lax.div(one, frames)
        perms[i] = jnp.where(source == other, 1.0, 0.0).astype(bf16)

    gz[z] = gs[...]
    if z_count > 1:
        wait_bytes(gz.at[pl.ds(0, z_count - 1)], gain_recv.at[0])
        wait_bytes(gz.at[pl.ds(0, z_count - 1)], gain_send.at[0])
    gs[...] = jnp.sum(gz[...], axis=0)
    loop(
        1, X,
        lambda d: remote(
            gs, gx.at[x], gain_send.at[1], gain_recv.at[1], {"grp": lax.rem(x + d, X) * z_count + z}
        ).start(),
    )
    gx[x] = gs[...]

    def halo(c, way):
        return remote(
            win.at[c, 0], win.at[c, 1 + way], halo_send.at[c, way], halo_recv.at[c, way],
            {"grp": lax.rem(grp + (1, group_count - 1)[way], group_count)},
        )

    def to_neighbours(c):
        wait_bytes(win.at[c, 0], recv_sem.at[c])
        for way in range(2):
            halo(c, way).start()

    def attend(c, between):
        lanes_of = [slice(h * HEAD_DIM, (h + 1) * HEAD_DIM) for h in range(CHUNK_HEADS)]
        gain_of = [
            [gains[a : a + 1, c * CH + h * HEAD_DIM : c * CH + (h + 1) * HEAD_DIM] for a in range(2)]
            for h in range(CHUNK_HEADS)
        ]

        def gather(slot):
            for a in range(4):
                moved = dot(perms[0], win[c, slot, a].reshape(rows, CH), ((1,), (0,)))
                for h in range(CHUNK_HEADS):
                    part = moved[:, lanes_of[h]]
                    if a < 2:
                        inverse = lax.rsqrt(mean_lanes(part * part) + EPS)
                        normed[a, h, slot] = (part * inverse * gain_of[h][a]).astype(bf16)

                        if isinstance(slot, int):
                            held[a, h] = part
                    else:
                        normed[a, h, slot] = part.astype(bf16)

        gather(0)
        for way in range(2):
            halo(c, way).wait_recv()
        loop(1, 3, gather)
        between[0]()

        def block(b, sums):
            at = pl.ds(pl.multiple_of(b * wide, wide), wide)
            live = jnp.where(limit[...] > y * POS + b * BLOCK_POS, 1.0, 0.0)
            new = []
            for h in range(CHUNK_HEADS):
                query, key, value, cotangent = (
                    normed[a, h, :, at, :].reshape(3 * wide, HEAD_DIM) for a in range(4)
                )
                scores = dot(query, key, ((1,), (1,))) * SCALE + bias[...]
                prob_grad = dot(cotangent, value, ((1,), (1,)))
                spread = jnp.exp(scores - jnp.max(scores, axis=-1, keepdims=True))
                probs = spread * (live / jnp.sum(spread, axis=-1, keepdims=True))
                rounded = probs.astype(bf16)
                attended = dot(rounded, value, ((1,), (0,))).astype(bf16)
                delta = jnp.sum(cotangent.astype(f32) * attended.astype(f32), axis=-1, keepdims=True)
                score_grad = (probs * (prob_grad - delta) * SCALE).astype(bf16)
                back[0, at, lanes_of[h]] = attended[:wide]
                back[3, at, lanes_of[h]] = dot(rounded[:, :wide], cotangent, ((0,), (0,))).astype(bf16)
                ups = (
                    dot(score_grad[:wide], key, ((1,), (0,))),
                    dot(score_grad[:, :wide], query, ((0,), (0,))),
                )
                for a in range(2):
                    up = ups[a].astype(bf16).astype(f32)
                    rows_in = held[a, h, at, :]
                    inverse = lax.rsqrt(mean_lanes(rows_in * rows_in) + EPS)
                    weighted = up * gain_of[h][a]
                    along = mean_lanes(weighted * rows_in)
                    scaled = rows_in * inverse
                    back[1 + a, at, lanes_of[h]] = (
                        inverse * weighted - scaled * inverse * inverse * along
                    ).astype(bf16)
                    new.append(sums[len(new)] + jnp.sum(up * scaled, axis=0, keepdims=True))
            return tuple(new)

        zero = jnp.zeros((1, HEAD_DIM), f32)
        sums = lax.fori_loop(0, POS // BLOCK_POS, block, (zero,) * (2 * CHUNK_HEADS))
        between[1]()
        for a in range(4):
            out = dot(perms[1], back[a], ((1,), (0,))).astype(bf16).reshape(frames, POS, CH)
            if a == 0:
                att[c, pl.ds(0, frames)] = out
            else:
                ret[c, a - 1] = out
        at_row = iota((POS, CH), 0)
        packed = jnp.zeros((POS, CH), f32)
        for a in range(2):
            packed = packed + hi_lo(jnp.concatenate(sums[a::2], axis=1), at_row, 2 * a)
        att[c, frames] = packed.astype(bf16)

    neighbours = (lax.rem(y + 1, y_count) * CORES + core, lax.rem(y + y_count - 1, y_count) * CORES + core)
    sibling = y * CORES + 1 - core
    first_part = (frames + 1) // 2
    halves = ((0, first_part), (first_part, frames + 1 - first_part))

    def ring_copy(c, way, hop, ref=None):
        at = lax.rem(y + hop * (y_count - 1 if way == 0 else 1), y_count)
        src, dst = ag.at[c, core, at], ag.at[c, core, at]
        if ref is not None:
            src = ref
        if hop + 1 == far:
            src, dst = src.at[pl.ds(*halves[way])], dst.at[pl.ds(*halves[way])]
        return remote(src, dst, ring_send.at[c, way, hop], ring_recv.at[c, way, hop], {"seq": neighbours[way]})

    def to_sibling(c, src, dst):
        remote(src, dst, sib_send.at[c], sib_recv.at[c], {"seq": sibling}).start()

    def ring_step(c, hop):
        for way in range(2):
            at = lax.rem(y + (hop + 1) * (y_count - 1 if way == 0 else 1), y_count)
            ref = ag.at[c, core, at]
            if hop + 1 == far:
                ref = ref.at[pl.ds(*halves[way])]
            wait_bytes(ref, ring_recv.at[c, way, hop])
            if hop + 1 < far:
                ring_copy(c, way, hop + 1).start()
            to_sibling(c, ref, ref)

    def ring_start(c):
        for way in range(2):
            ring_copy(c, way, 0, att.at[c]).start()
        to_sibling(c, att.at[c], ag.at[c, core, y])
        pltpu.make_async_copy(att.at[c], ag.at[c, core, y], own_sem.at[c]).start()

    def give_back(c, low, high):
        mine = rows_out.at[pl.ds(0, 3), y, :, pl.ds(pl.multiple_of(core * HALF + c * CH, HEAD_DIM), CH)]

        def send(i):
            odd = lax.rem(i, 2)
            other = lax.rem(seq + odd * lax.div(i + 1, 2) + (1 - odd) * (seq_count - lax.div(i, 2)), seq_count)
            remote(ret.at[c, :, other], mine, ret_send.at[c], ret_recv, {"seq": other}).start()

        if low == 0:
            pltpu.make_async_copy(ret.at[c, :, seq], mine, ret_recv).start()
        loop(max(low, 1), high, send)

    units = 2 * z_count
    turn[...] = jnp.zeros_like(turn)

    def weigh(c):
        wait_bytes(ag.at[c, core, y], own_sem.at[c])
        wait_bytes(ag.at[c, 1 - core], sib_recv.at[c])
        for kc in range(CORES):
            pltpu.make_async_copy(
                ag.at[c, kc, :, seq], rows_out.at[3, :, :, pl.ds(kc * HALF + c * CH, CH)], ret_recv
            ).start()
            right = jnp.concatenate([ag[c, kc, :, f].reshape(patches, CH) for f in range(frames)], axis=0)
            turn[pl.ds(0, width)] = dot(tokens[...], right, ((1,), (0,)))
            terms = jnp.sum(ag[c, kc, :, frames].astype(f32), axis=0)
            at_row = iota((POS, CH), 0)
            packed = hi_lo(terms[0:1] + terms[1:2], at_row, 0) + hi_lo(terms[2:3] + terms[3:4], at_row, 2)
            turn[pl.ds(width, POS)] = packed
            zall[kc, pl.ds(c * CH, CH)] = turn[...].T.astype(bf16)
        for unit in range(units * c // CHUNKS, units * (c + 1) // CHUNKS):
            for kc in range(CORES):
                owner = (2 * kc + unit // z_count) * z_count + unit % z_count

                @pl.when(grp != owner)
                def _(kc=kc, unit=unit, owner=owner):
                    remote(
                        zall.at[kc, pl.ds(unit * share, share)], shares.at[grp], share_send, share_recv, {"grp": owner}
                    ).start()

    def project():
        def frame_pair(i):
            left = jnp.concatenate(
                [
                    jnp.concatenate(
                        [ag[c, kc, :, 2 * i + j].reshape(patches, CH) for kc in range(CORES) for c in range(CHUNKS)], axis=1
                    )
                    for j in range(2)
                ],
                axis=0,
            )
            total = dot(w[...], left, ((1,), (1,))).astype(bf16)
            for j in range(2):
                proj_out[2 * i + j] = total[:, j * patches : (j + 1) * patches]

        loop(0, frames // 2, frame_pair)

    def part(eighths):
        return seq_count * eighths // 8

    def run(*events):
        def go():
            for event, c, *more in events:
                if event == "step" and more[0] < far:
                    ring_step(c, *more)
                elif event == "ring":
                    ring_start(c)
                elif event == "ret":
                    give_back(c, part(more[0]), part(more[1]))
                elif event == "weigh":
                    weigh(c)

        return go

    nothing = run()
    to_neighbours(0)
    wait_bytes(gx.at[pl.ds(0, X - 1)], gain_recv.at[1])
    gains[...] = jnp.sum(gx[...], axis=0)
    to_neighbours(1)
    attend(0, (nothing, nothing))
    run(("ring", 0), ("ret", 0, 0, 4))()
    to_neighbours(2)
    attend(1, (run(("step", 0, 0), ("ret", 0, 4, 8)), nothing))
    run(("ring", 1), ("step", 0, 1))()
    attend(2, (run(("step", 0, 2), ("step", 1, 0)), nothing))
    run(("ring", 2), ("step", 0, 3), ("step", 1, 1), ("step", 2, 0), ("ret", 1, 0, 4))()
    for load in (pltpu.make_async_copy(tokens, tokens, load_sem.at[4]), pltpu.make_async_copy(weight, w, load_sem.at[5])):
        load.wait()
    run(("weigh", 0), ("step", 1, 2), ("step", 2, 1), ("ret", 1, 4, 6), ("step", 1, 3), ("step", 2, 2), ("ret", 1, 6, 8), ("weigh", 1), ("step", 2, 3), ("weigh", 2), ("ret", 2, 0, 8))()
    project()
    own_unit = lax.rem(x, 2) * z_count + z
    shares[grp] = zall[lax.div(x, 2), pl.ds(pl.multiple_of(own_unit * share, POS), share)]
    wait_bytes(shares.at[pl.ds(0, group_count - 1)], share_recv)
    token_root = float(frames * patches * group_count) ** 0.5
    total = jnp.sum(shares[...].astype(f32), axis=0) / token_root
    wide_out[...] = total[:, :width]
    terms = total.T
    gain_out[0:1] = terms[width : width + 1] + terms[width + 1 : width + 2]
    gain_out[1:2] = terms[width + 2 : width + 3] + terms[width + 3 : width + 4]
    for c in range(CHUNKS):
        wait_bytes(win.at[c, 0, :, pl.ds(0, seq_count - 1)], send_sem.at[c])
        wait_bytes(ret.at[c, :, pl.ds(0, seq_count - 1)], ret_send.at[c])
        wait_bytes(ag.at[c, core], sib_send.at[c])
        for way in range(2):
            halo(c, way).wait_send()
            for hop in range(far):
                ring_copy(c, way, hop).wait_send()
    wait_bytes(gx.at[pl.ds(0, X - 1)], gain_send.at[1])
    wait_bytes(shares.at[pl.ds(0, group_count - 1)], share_send)
    wait_bytes(rows_out, ret_recv)


def hand_out_kernel(rows_in, proj_in, wide_in, gain_in, *rest):
    outs, sem = rest[:-1], rest[-1]
    copies = [pltpu.make_async_copy(rows_in.at[i], outs[i], sem.at[i]) for i in range(4)]
    copies.append(pltpu.make_async_copy(proj_in, outs[4], sem.at[4]))
    for copy in copies:
        copy.start()
    outs[5][...] = wide_in[...]
    for i in range(2):
        outs[6 + i][...] = gain_in[i]
    for copy in copies:
        copy.wait()


def body(
    query_rows,
    key_rows,
    value_rows,
    out_grad,
    proj_grad,
    proj_weight,
    query_gain,
    key_gain,
    clip_of_frame,
    patch_count,
):
    bf16, f32 = jnp.bfloat16, jnp.float32
    patches, channels = query_rows.shape[1:]
    seq_count, group_count = lax.axis_size("seq"), lax.axis_size("grp")
    y_count, z_count = seq_count // CORES, group_count // X
    frames = seq_count
    width = proj_weight.shape[0]
    share = channels // group_count
    rows = frames * POS
    wide = BLOCK_POS * frames
    far = y_count // 2
    vmem, anywhere = pl.BlockSpec(memory_space=pltpu.VMEM), pl.BlockSpec(memory_space=pl.ANY)
    dma = pltpu.SemaphoreType.DMA
    rows_out, projected, wide_out, gain_out = pl.pallas_call(
        fused_kernel,
        out_shape=(
            jax.ShapeDtypeStruct((4, y_count, POS, channels), bf16),
            jax.ShapeDtypeStruct((frames, width, patches), bf16),
            jax.ShapeDtypeStruct((share, width), f32),
            jax.ShapeDtypeStruct((2, share), f32),
        ),
        in_specs=[pl.BlockSpec(memory_space=pltpu.HBM)] * 10,
        out_specs=(anywhere, vmem, vmem, vmem),
        scratch_shapes=[
            pltpu.VMEM((4, y_count, POS, channels), bf16),
            pltpu.VMEM((CHUNKS, 3, 4, frames, POS, CH), bf16),
            pltpu.VMEM((4, CHUNK_HEADS, 3, rows, HEAD_DIM), bf16),
            pltpu.VMEM((2, CHUNK_HEADS, rows, HEAD_DIM), f32),
            pltpu.VMEM((3 * wide, 3 * wide), f32),
            pltpu.VMEM((3 * wide, 1), jnp.int32),
            pltpu.VMEM((2, rows, rows), bf16),
            pltpu.VMEM((4, rows, CH), bf16),
            pltpu.VMEM((CHUNKS, 3, frames, POS, CH), bf16),
            pltpu.VMEM((CHUNKS, frames + 1, POS, CH), bf16),
            pltpu.VMEM((CHUNKS, CORES, y_count, frames + 1, POS, CH), bf16),
            pltpu.VMEM((width, frames * patches), bf16),
            pltpu.VMEM((width, channels), bf16),
            pltpu.VMEM((LANES, CH), f32),
            pltpu.VMEM((CORES, HALF, LANES), bf16),
            pltpu.VMEM((group_count, share, LANES), bf16),
            pltpu.VMEM((z_count, 8, HALF), f32),
            pltpu.VMEM((X, 8, HALF), f32),
            pltpu.VMEM((8, HALF), f32),
            pltpu.VMEM((8, HALF), f32),
            pltpu.SMEM((share,), f32),
            pltpu.SMEM((share,), f32),
            pltpu.SMEM(clip_of_frame.shape, jnp.int32),
            pltpu.SMEM(patch_count.shape, jnp.int32),
            dma((10,)),
            dma((CHUNKS,)),
            dma((CHUNKS,)),
            dma((CHUNKS, 2)),
            dma((CHUNKS, 2)),
            dma((2,)),
            dma((2,)),
            dma((CHUNKS,)),
            dma,
            dma((CHUNKS,)),
            dma((CHUNKS, 2, far)),
            dma((CHUNKS, 2, far)),
            dma((CHUNKS,)),
            dma((CHUNKS,)),
            dma,
            dma,
        ],
        compiler_params=pltpu.CompilerParams(collective_id=0, has_side_effects=True, vmem_limit_bytes=VMEM_LIMIT),
        name="fused",
    )(
        *(
            pltpu.with_memory_space_constraint(a, pltpu.HBM)
            for a in (
                *(a.reshape(y_count, POS, channels) for a in (query_rows, key_rows, value_rows, out_grad)),
                query_gain, key_gain, clip_of_frame, patch_count, proj_grad, proj_weight,
            )
        )
    )
    by_position = jax.ShapeDtypeStruct((y_count, POS, channels), bf16)
    outs = pl.pallas_call(
        hand_out_kernel,
        out_shape=(by_position,) * 4
        + (
            jax.ShapeDtypeStruct(projected.shape, bf16),
            jax.ShapeDtypeStruct(wide_out.shape, f32),
            jax.ShapeDtypeStruct((share,), f32),
            jax.ShapeDtypeStruct((share,), f32),
        ),
        in_specs=[vmem] * 4,
        out_specs=(anywhere,) * 5 + (vmem,) * 3,
        scratch_shapes=[dma((5,))],
        compiler_params=pltpu.CompilerParams(vmem_limit_bytes=VMEM_LIMIT),
        name="hand_out",
    )(rows_out, projected, wide_out, gain_out)
    query_grad, key_grad, value_grad, attended = (rows.reshape(1, patches, channels) for rows in outs[:4])
    return attended, outs[4], query_grad, key_grad, value_grad, *outs[5:]


def solution(mesh):
    rows = P(("grp", "seq"), None, None)
    in_specs = (rows, rows, rows, rows, P("grp", "seq", None), P("seq", None), P("grp"), P("grp"), P(), P())
    out_specs = (rows, P("grp", "seq", None), rows, rows, rows, P("grp", "seq"), P("grp"), P("grp"))
    return jax.shard_map(body, mesh=mesh, in_specs=in_specs, out_specs=out_specs, check_vma=False)
```

```python
import jax
import jax.numpy as jnp
from jax import lax
from jax.experimental import pallas as pl
from jax.experimental.pallas import tpu as pltpu
from jax.sharding import PartitionSpec as P

HEADS = 12
HEAD_DIM = 128
EPS = 1e-06
NEGATIVE = -1e30
SCALE = HEAD_DIM ** (-0.5)
MESH = pl.DeviceIdType.MESH

POS = 16
CORES = 2
CHUNKS = 3
CHUNK_HEADS = HEADS // (CORES * CHUNKS)
CH = CHUNK_HEADS * HEAD_DIM
HALF = CHUNKS * CH
X = 4
BLOCK_POS = 8
LANES = 256
VMEM_LIMIT = 28 * 1024 * 1024


def dot(a, b, dims):
    return lax.dot_general(a, b, (dims, ((), ())), preferred_element_type=jnp.float32)


def place():
    seq_count = lax.axis_size("seq")
    group_count = lax.axis_size("grp")
    grp, seq = lax.axis_index("grp"), lax.axis_index("seq")
    z_count, y_count = group_count // X, seq_count // CORES
    return (
        grp, seq, z_count, y_count,
        lax.div(grp, z_count), lax.rem(grp, z_count),
        lax.div(seq, CORES), lax.rem(seq, CORES),
    )


def wait_bytes(ref, sem):
    pltpu.make_async_copy(ref, ref, sem).wait()


def remote(src, dst, send_sem, recv_sem, device):
    return pltpu.make_async_remote_copy(
        src_ref=src, dst_ref=dst, send_sem=send_sem, recv_sem=recv_sem, device_id=device, device_id_type=MESH
    )


def loop(low, high, step):
    def one(i, carry):
        step(i)
        return carry

    lax.fori_loop(low, high, one, 0)


def greet():
    grp, seq, z_count, y_count, x, z, y, core = place()
    seq_count, group_count = y_count * CORES, z_count * X
    barrier = pltpu.get_barrier_semaphore()

    def signal(device):
        pl.semaphore_signal(barrier, inc=1, device_id=device, device_id_type=MESH)

    loop(1, seq_count, lambda d: signal({"seq": lax.rem(seq + d, seq_count)}))
    loop(1, group_count, lambda d: signal({"grp": lax.rem(grp + d, group_count)}))
    return lambda: pl.semaphore_wait(barrier, seq_count + group_count - 2)


def mean_lanes(values):
    return jnp.mean(values, axis=-1, keepdims=True)


def hi_lo(total, row, first):
    high = total.astype(jnp.bfloat16).astype(jnp.float32)
    low = total - high
    return jnp.where(row == first, high, 0.0) + jnp.where(row == first + 1, low, 0.0)


def iota(shape, dim):
    return lax.broadcasted_iota(jnp.int32, shape, dim)


def fused_kernel(
    q, k, v, g, query_gain_in, key_gain_in, clip_in, count_in, grad, weight,
    rows_out, proj_out, wide_out, gain_out,
    stage, win, normed, held, bias, limit, perms, back, ret, att, ag, tokens, w, turn, zall, shares, gz, gx, gs, gains,
    query_gain, key_gain, clip, count,
    load_sem, send_sem, recv_sem, halo_send, halo_recv, gain_send, gain_recv,
    ret_send, ret_recv, own_sem, ring_send, ring_recv, sib_send, sib_recv, share_send, share_recv,
):
    grp, seq, z_count, y_count, x, z, y, core = place()
    seq_count, group_count = y_count * CORES, z_count * X
    frames, width, patches = grad.shape
    rows = frames * POS
    wide = BLOCK_POS * frames
    share = HALF * CORES // group_count
    far = y_count // 2
    f32, bf16 = jnp.float32, jnp.bfloat16

    greeted = greet()
    loads = [pltpu.make_async_copy(ref, stage.at[i], load_sem.at[i]) for i, ref in enumerate((q, k, v, g))]
    for load in loads:
        load.start()
    small = [
        pltpu.make_async_copy(ref, held_ref, load_sem.at[6 + i])
        for i, (ref, held_ref) in enumerate(
            ((query_gain_in, query_gain), (key_gain_in, key_gain), (clip_in, clip), (count_in, count))
        )
    ]
    for load in small:
        load.start()
    greeted()

    for load in loads:
        load.wait()
    for c in range(CHUNKS):
        def spread_out(i, c=c):
            odd = lax.rem(i, 2)
            dy = odd * lax.div(i + 1, 2) + (1 - odd) * (y_count - lax.div(i, 2))
            other = lax.rem(y + dy, y_count)
            for cc in range(CORES):
                remote(
                    stage.at[:, other, :, pl.ds(cc * HALF + c * CH, CH)], win.at[c, 0, :, seq],
                    send_sem.at[c], recv_sem.at[c], {"seq": other * CORES + cc},
                ).start()

        loop(1, y_count, spread_out)
        remote(
            stage.at[:, y, :, pl.ds(pl.multiple_of((1 - core) * HALF + c * CH, HEAD_DIM), CH)],
            win.at[c, 0, :, seq], send_sem.at[c], recv_sem.at[c], {"seq": y * CORES + 1 - core},
        ).start()
        pltpu.make_async_copy(
            stage.at[:, y, :, pl.ds(pl.multiple_of(core * HALF + c * CH, HEAD_DIM), CH)],
            win.at[c, 0, :, seq], recv_sem.at[c],
        ).start()

    for f in range(frames):
        pltpu.make_async_copy(grad.at[f], tokens.at[:, pl.ds(f * patches, patches)], load_sem.at[4]).start()
    pltpu.make_async_copy(weight, w, load_sem.at[5]).start()
    for load in small:
        load.wait()

    lane, sub = iota((8, HALF), 1), iota((8, HALF), 0)
    gs[...] = jnp.zeros_like(gs)

    def put_gain(i):
        at = lane == grp * share + i - core * HALF
        gs[...] += jnp.where(at & (sub == 0), query_gain[i], 0.0) + jnp.where(at & (sub == 1), key_gain[i], 0.0)

    loop(0, share, put_gain)
    if z_count > 1:
        loop(
            1, z_count,
            lambda d: remote(
                gs, gz.at[z], gain_send.at[0], gain_recv.at[0], {"grp": x * z_count + lax.rem(z + d, z_count)}
            ).start(),
        )
    def code_of(index, slot):
        at = (grp + (0, -1, 1)[slot]) * frames + index
        inside = (at >= 0) & (at < frames * group_count)
        own_clip = clip[lax.rem(at + frames * group_count, frames * group_count)]
        return jnp.where(inside, own_clip, -1), jnp.where(inside, count[own_clip], 0)

    col, row = iota((3 * wide, 1), 0), iota((1, 3 * wide), 1)
    col_code, row_code = jnp.zeros((3 * wide, 1), jnp.int32), jnp.zeros((1, 3 * wide), jnp.int32)
    col_count = jnp.zeros((3 * wide, 1), jnp.int32)
    for slot in range(3):
        def put_code(i, carry, slot=slot):
            col_code, row_code, col_count = carry
            code, most = code_of(i, slot)

            def here(index):
                return (lax.div(index, wide) == slot) & (lax.rem(index, frames) == i)

            return (
                jnp.where(here(col), code, col_code),
                jnp.where(here(row), code, row_code),
                jnp.where(here(col), most, col_count),
            )

        col_code, row_code, col_count = lax.fori_loop(0, frames, put_code, (col_code, row_code, col_count))

    def position(index):
        return lax.div(lax.rem(index, wide), frames)

    bias[...] = jnp.where((col_code == row_code) & (position(col) == position(row)), 0.0, NEGATIVE)
    limit[...] = col_count - position(col)
    down, across = iota((rows, rows), 0), iota((rows, rows), 1)
    for i, (one, other) in enumerate(((down, across), (across, down))):
        source = lax.rem(one, frames) * POS + lax.div(one, frames)
        perms[i] = jnp.where(source == other, 1.0, 0.0).astype(bf16)

    gz[z] = gs[...]
    if z_count > 1:
        wait_bytes(gz.at[pl.ds(0, z_count - 1)], gain_recv.at[0])
        wait_bytes(gz.at[pl.ds(0, z_count - 1)], gain_send.at[0])
    gs[...] = jnp.sum(gz[...], axis=0)
    loop(
        1, X,
        lambda d: remote(
            gs, gx.at[x], gain_send.at[1], gain_recv.at[1], {"grp": lax.rem(x + d, X) * z_count + z}
        ).start(),
    )
    gx[x] = gs[...]

    def halo(c, way):
        return remote(
            win.at[c, 0], win.at[c, 1 + way], halo_send.at[c, way], halo_recv.at[c, way],
            {"grp": lax.rem(grp + (1, group_count - 1)[way], group_count)},
        )

    def to_neighbours(c):
        wait_bytes(win.at[c, 0], recv_sem.at[c])
        for way in range(2):
            halo(c, way).start()

    def attend(c, between):
        lanes_of = [slice(h * HEAD_DIM, (h + 1) * HEAD_DIM) for h in range(CHUNK_HEADS)]
        gain_of = [
            [gains[a : a + 1, c * CH + h * HEAD_DIM : c * CH + (h + 1) * HEAD_DIM] for a in range(2)]
            for h in range(CHUNK_HEADS)
        ]

        def gather(slot):
            for a in range(4):
                moved = dot(perms[0], win[c, slot, a].reshape(rows, CH), ((1,), (0,)))
                for h in range(CHUNK_HEADS):
                    part = moved[:, lanes_of[h]]
                    if a < 2:
                        inverse = lax.rsqrt(mean_lanes(part * part) + EPS)
                        normed[a, h, slot] = (part * inverse * gain_of[h][a]).astype(bf16)

                        if isinstance(slot, int):
                            held[a, h] = part
                    else:
                        normed[a, h, slot] = part.astype(bf16)

        gather(0)
        for way in range(2):
            halo(c, way).wait_recv()
        loop(1, 3, gather)
        between[0]()

        def block(b, sums):
            at = pl.ds(pl.multiple_of(b * wide, wide), wide)
            live = jnp.where(limit[...] > y * POS + b * BLOCK_POS, 1.0, 0.0)
            new = []
            for h in range(CHUNK_HEADS):
                query, key, value, cotangent = (
                    normed[a, h, :, at, :].reshape(3 * wide, HEAD_DIM) for a in range(4)
                )
                scores = dot(query, key, ((1,), (1,))) * SCALE + bias[...]
                prob_grad = dot(cotangent, value, ((1,), (1,)))
                spread = jnp.exp(scores - jnp.max(scores, axis=-1, keepdims=True))
                probs = spread * (live / jnp.sum(spread, axis=-1, keepdims=True))
                rounded = probs.astype(bf16)
                attended = dot(rounded, value, ((1,), (0,))).astype(bf16)
                delta = jnp.sum(cotangent.astype(f32) * attended.astype(f32), axis=-1, keepdims=True)
                score_grad = (probs * (prob_grad - delta) * SCALE).astype(bf16)
                back[0, at, lanes_of[h]] = attended[:wide]
                back[3, at, lanes_of[h]] = dot(rounded[:, :wide], cotangent, ((0,), (0,))).astype(bf16)
                ups = (
                    dot(score_grad[:wide], key, ((1,), (0,))),
                    dot(score_grad[:, :wide], query, ((0,), (0,))),
                )
                for a in range(2):
                    up = ups[a].astype(bf16).astype(f32)
                    rows_in = held[a, h, at, :]
                    inverse = lax.rsqrt(mean_lanes(rows_in * rows_in) + EPS)
                    weighted = up * gain_of[h][a]
                    along = mean_lanes(weighted * rows_in)
                    scaled = rows_in * inverse
                    back[1 + a, at, lanes_of[h]] = (
                        inverse * weighted - scaled * inverse * inverse * along
                    ).astype(bf16)
                    new.append(sums[len(new)] + jnp.sum(up * scaled, axis=0, keepdims=True))
            return tuple(new)

        zero = jnp.zeros((1, HEAD_DIM), f32)
        sums = lax.fori_loop(0, POS // BLOCK_POS, block, (zero,) * (2 * CHUNK_HEADS))
        between[1]()
        for a in range(4):
            out = dot(perms[1], back[a], ((1,), (0,))).astype(bf16).reshape(frames, POS, CH)
            if a == 0:
                att[c, pl.ds(0, frames)] = out
            else:
                ret[c, a - 1] = out
        at_row = iota((POS, CH), 0)
        packed = jnp.zeros((POS, CH), f32)
        for a in range(2):
            packed = packed + hi_lo(jnp.concatenate(sums[a::2], axis=1), at_row, 2 * a)
        att[c, frames] = packed.astype(bf16)

    neighbours = (lax.rem(y + 1, y_count) * CORES + core, lax.rem(y + y_count - 1, y_count) * CORES + core)
    sibling = y * CORES + 1 - core
    first_part = (frames + 1) // 2
    halves = ((0, first_part), (first_part, frames + 1 - first_part))

    def ring_copy(c, way, hop, ref=None):
        at = lax.rem(y + hop * (y_count - 1 if way == 0 else 1), y_count)
        src, dst = ag.at[c, core, at], ag.at[c, core, at]
        if ref is not None:
            src = ref
        if hop + 1 == far:
            src, dst = src.at[pl.ds(*halves[way])], dst.at[pl.ds(*halves[way])]
        return remote(src, dst, ring_send.at[c, way, hop], ring_recv.at[c, way, hop], {"seq": neighbours[way]})

    def to_sibling(c, src, dst):
        remote(src, dst, sib_send.at[c], sib_recv.at[c], {"seq": sibling}).start()

    def ring_step(c, hop):
        for way in range(2):
            at = lax.rem(y + (hop + 1) * (y_count - 1 if way == 0 else 1), y_count)
            ref = ag.at[c, core, at]
            if hop + 1 == far:
                ref = ref.at[pl.ds(*halves[way])]
            wait_bytes(ref, ring_recv.at[c, way, hop])
            if hop + 1 < far:
                ring_copy(c, way, hop + 1).start()
            to_sibling(c, ref, ref)

    def ring_start(c):
        for way in range(2):
            ring_copy(c, way, 0, att.at[c]).start()
        to_sibling(c, att.at[c], ag.at[c, core, y])
        pltpu.make_async_copy(att.at[c], ag.at[c, core, y], own_sem.at[c]).start()

    def give_back(c, low, high):
        mine = rows_out.at[pl.ds(0, 3), y, :, pl.ds(pl.multiple_of(core * HALF + c * CH, HEAD_DIM), CH)]

        def send(i):
            odd = lax.rem(i, 2)
            other = lax.rem(seq + odd * lax.div(i + 1, 2) + (1 - odd) * (seq_count - lax.div(i, 2)), seq_count)
            remote(ret.at[c, :, other], mine, ret_send.at[c], ret_recv, {"seq": other}).start()

        if low == 0:
            pltpu.make_async_copy(ret.at[c, :, seq], mine, ret_recv).start()
        loop(max(low, 1), high, send)

    units = 2 * z_count
    turn[...] = jnp.zeros_like(turn)

    def weigh(c):
        wait_bytes(ag.at[c, core, y], own_sem.at[c])
        wait_bytes(ag.at[c, 1 - core], sib_recv.at[c])
        for kc in range(CORES):
            pltpu.make_async_copy(
                ag.at[c, kc, :, seq], rows_out.at[3, :, :, pl.ds(kc * HALF + c * CH, CH)], ret_recv
            ).start()
            right = jnp.concatenate([ag[c, kc, :, f].reshape(patches, CH) for f in range(frames)], axis=0)
            turn[pl.ds(0, width)] = dot(tokens[...], right, ((1,), (0,)))
            terms = jnp.sum(ag[c, kc, :, frames].astype(f32), axis=0)
            at_row = iota((POS, CH), 0)
            packed = hi_lo(terms[0:1] + terms[1:2], at_row, 0) + hi_lo(terms[2:3] + terms[3:4], at_row, 2)
            turn[pl.ds(width, POS)] = packed
            zall[kc, pl.ds(c * CH, CH)] = turn[...].T.astype(bf16)
        for unit in range(units * c // CHUNKS, units * (c + 1) // CHUNKS):
            for kc in range(CORES):
                owner = (2 * kc + unit // z_count) * z_count + unit % z_count

                @pl.when(grp != owner)
                def _(kc=kc, unit=unit, owner=owner):
                    remote(
                        zall.at[kc, pl.ds(unit * share, share)], shares.at[grp], share_send, share_recv, {"grp": owner}
                    ).start()

    def project():
        def frame_pair(i):
            left = jnp.concatenate(
                [
                    jnp.concatenate(
                        [ag[c, kc, :, 2 * i + j].reshape(patches, CH) for kc in range(CORES) for c in range(CHUNKS)], axis=1
                    )
                    for j in range(2)
                ],
                axis=0,
            )
            total = dot(w[...], left, ((1,), (1,))).astype(bf16)
            for j in range(2):
                proj_out[2 * i + j] = total[:, j * patches : (j + 1) * patches]

        loop(0, frames // 2, frame_pair)

    def part(eighths):
        return seq_count * eighths // 8

    def run(*events):
        def go():
            for event, c, *more in events:
                if event == "step" and more[0] < far:
                    ring_step(c, *more)
                elif event == "ring":
                    ring_start(c)
                elif event == "ret":
                    give_back(c, part(more[0]), part(more[1]))
                elif event == "weigh":
                    weigh(c)

        return go

    nothing = run()
    to_neighbours(0)
    wait_bytes(gx.at[pl.ds(0, X - 1)], gain_recv.at[1])
    gains[...] = jnp.sum(gx[...], axis=0)
    to_neighbours(1)
    attend(0, (nothing, nothing))
    run(("ring", 0), ("ret", 0, 0, 8))()
    to_neighbours(2)
    attend(1, (run(("step", 0, 0)), nothing))
    run(("ring", 1), ("step", 0, 1))()
    attend(2, (run(("step", 0, 2), ("step", 1, 0)), run(("ret", 1, 0, 3), ("step", 0, 3))))
    run(("ring", 2), ("step", 1, 1), ("ret", 1, 3, 5), ("step", 2, 0))()
    for load in (pltpu.make_async_copy(tokens, tokens, load_sem.at[4]), pltpu.make_async_copy(weight, w, load_sem.at[5])):
        load.wait()
    run(("weigh", 0), ("ret", 1, 5, 6), ("step", 1, 2), ("step", 2, 1), ("ret", 1, 6, 8), ("step", 1, 3), ("weigh", 1), ("step", 2, 2), ("ret", 2, 0, 4), ("step", 2, 3), ("weigh", 2), ("ret", 2, 4, 8))()
    project()
    own_unit = lax.rem(x, 2) * z_count + z
    shares[grp] = zall[lax.div(x, 2), pl.ds(pl.multiple_of(own_unit * share, POS), share)]
    wait_bytes(shares.at[pl.ds(0, group_count - 1)], share_recv)
    token_root = float(frames * patches * group_count) ** 0.5
    total = jnp.sum(shares[...].astype(f32), axis=0) / token_root
    wide_out[...] = total[:, :width]
    terms = total.T
    gain_out[0:1] = terms[width : width + 1] + terms[width + 1 : width + 2]
    gain_out[1:2] = terms[width + 2 : width + 3] + terms[width + 3 : width + 4]
    for c in range(CHUNKS):
        wait_bytes(win.at[c, 0, :, pl.ds(0, seq_count - 1)], send_sem.at[c])
        wait_bytes(ret.at[c, :, pl.ds(0, seq_count - 1)], ret_send.at[c])
        wait_bytes(ag.at[c, core], sib_send.at[c])
        for way in range(2):
            halo(c, way).wait_send()
            for hop in range(far):
                ring_copy(c, way, hop).wait_send()
    wait_bytes(gx.at[pl.ds(0, X - 1)], gain_send.at[1])
    wait_bytes(shares.at[pl.ds(0, group_count - 1)], share_send)
    wait_bytes(rows_out, ret_recv)


def hand_out_kernel(rows_in, proj_in, wide_in, gain_in, *rest):
    outs, sem = rest[:-1], rest[-1]
    copies = [pltpu.make_async_copy(rows_in.at[i], outs[i], sem.at[i]) for i in range(4)]
    copies.append(pltpu.make_async_copy(proj_in, outs[4], sem.at[4]))
    for copy in copies:
        copy.start()
    outs[5][...] = wide_in[...]
    for i in range(2):
        outs[6 + i][...] = gain_in[i]
    for copy in copies:
        copy.wait()


def body(
    query_rows,
    key_rows,
    value_rows,
    out_grad,
    proj_grad,
    proj_weight,
    query_gain,
    key_gain,
    clip_of_frame,
    patch_count,
):
    bf16, f32 = jnp.bfloat16, jnp.float32
    patches, channels = query_rows.shape[1:]
    seq_count, group_count = lax.axis_size("seq"), lax.axis_size("grp")
    y_count, z_count = seq_count // CORES, group_count // X
    frames = seq_count
    width = proj_weight.shape[0]
    share = channels // group_count
    rows = frames * POS
    wide = BLOCK_POS * frames
    far = y_count // 2
    vmem, anywhere = pl.BlockSpec(memory_space=pltpu.VMEM), pl.BlockSpec(memory_space=pl.ANY)
    dma = pltpu.SemaphoreType.DMA
    rows_out, projected, wide_out, gain_out = pl.pallas_call(
        fused_kernel,
        out_shape=(
            jax.ShapeDtypeStruct((4, y_count, POS, channels), bf16),
            jax.ShapeDtypeStruct((frames, width, patches), bf16),
            jax.ShapeDtypeStruct((share, width), f32),
            jax.ShapeDtypeStruct((2, share), f32),
        ),
        in_specs=[pl.BlockSpec(memory_space=pltpu.HBM)] * 10,
        out_specs=(anywhere, vmem, vmem, vmem),
        scratch_shapes=[
            pltpu.VMEM((4, y_count, POS, channels), bf16),
            pltpu.VMEM((CHUNKS, 3, 4, frames, POS, CH), bf16),
            pltpu.VMEM((4, CHUNK_HEADS, 3, rows, HEAD_DIM), bf16),
            pltpu.VMEM((2, CHUNK_HEADS, rows, HEAD_DIM), f32),
            pltpu.VMEM((3 * wide, 3 * wide), f32),
            pltpu.VMEM((3 * wide, 1), jnp.int32),
            pltpu.VMEM((2, rows, rows), bf16),
            pltpu.VMEM((4, rows, CH), bf16),
            pltpu.VMEM((CHUNKS, 3, frames, POS, CH), bf16),
            pltpu.VMEM((CHUNKS, frames + 1, POS, CH), bf16),
            pltpu.VMEM((CHUNKS, CORES, y_count, frames + 1, POS, CH), bf16),
            pltpu.VMEM((width, frames * patches), bf16),
            pltpu.VMEM((width, channels), bf16),
            pltpu.VMEM((LANES, CH), f32),
            pltpu.VMEM((CORES, HALF, LANES), bf16),
            pltpu.VMEM((group_count, share, LANES), bf16),
            pltpu.VMEM((z_count, 8, HALF), f32),
            pltpu.VMEM((X, 8, HALF), f32),
            pltpu.VMEM((8, HALF), f32),
            pltpu.VMEM((8, HALF), f32),
            pltpu.SMEM((share,), f32),
            pltpu.SMEM((share,), f32),
            pltpu.SMEM(clip_of_frame.shape, jnp.int32),
            pltpu.SMEM(patch_count.shape, jnp.int32),
            dma((10,)),
            dma((CHUNKS,)),
            dma((CHUNKS,)),
            dma((CHUNKS, 2)),
            dma((CHUNKS, 2)),
            dma((2,)),
            dma((2,)),
            dma((CHUNKS,)),
            dma,
            dma((CHUNKS,)),
            dma((CHUNKS, 2, far)),
            dma((CHUNKS, 2, far)),
            dma((CHUNKS,)),
            dma((CHUNKS,)),
            dma,
            dma,
        ],
        compiler_params=pltpu.CompilerParams(collective_id=0, has_side_effects=True, vmem_limit_bytes=VMEM_LIMIT),
        name="fused",
    )(
        *(
            pltpu.with_memory_space_constraint(a, pltpu.HBM)
            for a in (
                *(a.reshape(y_count, POS, channels) for a in (query_rows, key_rows, value_rows, out_grad)),
                query_gain, key_gain, clip_of_frame, patch_count, proj_grad, proj_weight,
            )
        )
    )
    by_position = jax.ShapeDtypeStruct((y_count, POS, channels), bf16)
    outs = pl.pallas_call(
        hand_out_kernel,
        out_shape=(by_position,) * 4
        + (
            jax.ShapeDtypeStruct(projected.shape, bf16),
            jax.ShapeDtypeStruct(wide_out.shape, f32),
            jax.ShapeDtypeStruct((share,), f32),
            jax.ShapeDtypeStruct((share,), f32),
        ),
        in_specs=[vmem] * 4,
        out_specs=(anywhere,) * 5 + (vmem,) * 3,
        scratch_shapes=[dma((5,))],
        compiler_params=pltpu.CompilerParams(vmem_limit_bytes=VMEM_LIMIT),
        name="hand_out",
    )(rows_out, projected, wide_out, gain_out)
    query_grad, key_grad, value_grad, attended = (rows.reshape(1, patches, channels) for rows in outs[:4])
    return attended, outs[4], query_grad, key_grad, value_grad, *outs[5:]


def solution(mesh):
    rows = P(("grp", "seq"), None, None)
    in_specs = (rows, rows, rows, rows, P("grp", "seq", None), P("seq", None), P("grp"), P("grp"), P(), P())
    out_specs = (rows, P("grp", "seq", None), rows, rows, rows, P("grp", "seq"), P("grp"), P("grp"))
    return jax.shard_map(body, mesh=mesh, in_specs=in_specs, out_specs=out_specs, check_vma=False)
```

```python
import jax
import jax.numpy as jnp
from jax import lax
from jax.experimental import pallas as pl
from jax.experimental.pallas import tpu as pltpu
from jax.sharding import PartitionSpec as P

HEADS = 12
HEAD_DIM = 128
EPS = 1e-06
NEGATIVE = -1e30
SCALE = HEAD_DIM ** (-0.5)
MESH = pl.DeviceIdType.MESH

POS = 16
CORES = 2
CHUNKS = 3
CHUNK_HEADS = HEADS // (CORES * CHUNKS)
CH = CHUNK_HEADS * HEAD_DIM
HALF = CHUNKS * CH
X = 4
BLOCK_POS = 8
LANES = 256
VMEM_LIMIT = 28 * 1024 * 1024


def dot(a, b, dims):
    return lax.dot_general(a, b, (dims, ((), ())), preferred_element_type=jnp.float32)


def place():
    seq_count = lax.axis_size("seq")
    group_count = lax.axis_size("grp")
    grp, seq = lax.axis_index("grp"), lax.axis_index("seq")
    z_count, y_count = group_count // X, seq_count // CORES
    return (
        grp, seq, z_count, y_count,
        lax.div(grp, z_count), lax.rem(grp, z_count),
        lax.div(seq, CORES), lax.rem(seq, CORES),
    )


def wait_bytes(ref, sem):
    pltpu.make_async_copy(ref, ref, sem).wait()


def remote(src, dst, send_sem, recv_sem, device):
    return pltpu.make_async_remote_copy(
        src_ref=src, dst_ref=dst, send_sem=send_sem, recv_sem=recv_sem, device_id=device, device_id_type=MESH
    )


def loop(low, high, step):
    def one(i, carry):
        step(i)
        return carry

    lax.fori_loop(low, high, one, 0)


def greet():
    grp, seq, z_count, y_count, x, z, y, core = place()
    seq_count, group_count = y_count * CORES, z_count * X
    barrier = pltpu.get_barrier_semaphore()

    def signal(device):
        pl.semaphore_signal(barrier, inc=1, device_id=device, device_id_type=MESH)

    loop(1, seq_count, lambda d: signal({"seq": lax.rem(seq + d, seq_count)}))
    loop(1, group_count, lambda d: signal({"grp": lax.rem(grp + d, group_count)}))
    return lambda: pl.semaphore_wait(barrier, seq_count + group_count - 2)


def mean_lanes(values):
    return jnp.mean(values, axis=-1, keepdims=True)


def hi_lo(total, row, first):
    high = total.astype(jnp.bfloat16).astype(jnp.float32)
    low = total - high
    return jnp.where(row == first, high, 0.0) + jnp.where(row == first + 1, low, 0.0)


def iota(shape, dim):
    return lax.broadcasted_iota(jnp.int32, shape, dim)


def fused_kernel(
    q, k, v, g, query_gain_in, key_gain_in, clip_in, count_in, grad, weight,
    rows_out, proj_out, wide_out, gain_out,
    stage, win, normed, held, bias, limit, perms, back, ret, att, ag, tokens, w, turn, zall, shares, gz, gx, gs, gains,
    query_gain, key_gain, clip, count,
    load_sem, send_sem, recv_sem, halo_send, halo_recv, gain_send, gain_recv,
    ret_send, ret_recv, own_sem, ring_send, ring_recv, sib_send, sib_recv, share_send, share_recv,
):
    grp, seq, z_count, y_count, x, z, y, core = place()
    seq_count, group_count = y_count * CORES, z_count * X
    frames, width, patches = grad.shape
    rows = frames * POS
    wide = BLOCK_POS * frames
    share = HALF * CORES // group_count
    far = y_count // 2
    f32, bf16 = jnp.float32, jnp.bfloat16

    greeted = greet()
    loads = [pltpu.make_async_copy(ref, stage.at[i], load_sem.at[i]) for i, ref in enumerate((q, k, v, g))]
    for load in loads:
        load.start()
    small = [
        pltpu.make_async_copy(ref, held_ref, load_sem.at[6 + i])
        for i, (ref, held_ref) in enumerate(
            ((query_gain_in, query_gain), (key_gain_in, key_gain), (clip_in, clip), (count_in, count))
        )
    ]
    for load in small:
        load.start()
    greeted()

    for load in loads:
        load.wait()
    for c in range(CHUNKS):
        def spread_out(i, c=c):
            odd = lax.rem(i, 2)
            dy = odd * lax.div(i + 1, 2) + (1 - odd) * (y_count - lax.div(i, 2))
            other = lax.rem(y + dy, y_count)
            for cc in range(CORES):
                remote(
                    stage.at[:, other, :, pl.ds(cc * HALF + c * CH, CH)], win.at[c, 0, :, seq],
                    send_sem.at[c], recv_sem.at[c], {"seq": other * CORES + cc},
                ).start()

        loop(1, y_count, lambda i, spread_out=spread_out: spread_out(y_count - i))
        remote(
            stage.at[:, y, :, pl.ds(pl.multiple_of((1 - core) * HALF + c * CH, HEAD_DIM), CH)],
            win.at[c, 0, :, seq], send_sem.at[c], recv_sem.at[c], {"seq": y * CORES + 1 - core},
        ).start()
        pltpu.make_async_copy(
            stage.at[:, y, :, pl.ds(pl.multiple_of(core * HALF + c * CH, HEAD_DIM), CH)],
            win.at[c, 0, :, seq], recv_sem.at[c],
        ).start()

    for f in range(frames):
        pltpu.make_async_copy(grad.at[f], tokens.at[:, pl.ds(f * patches, patches)], load_sem.at[4]).start()
    pltpu.make_async_copy(weight, w, load_sem.at[5]).start()
    for load in small:
        load.wait()

    lane, sub = iota((8, HALF), 1), iota((8, HALF), 0)
    gs[...] = jnp.zeros_like(gs)

    def put_gain(i):
        at = lane == grp * share + i - core * HALF
        gs[...] += jnp.where(at & (sub == 0), query_gain[i], 0.0) + jnp.where(at & (sub == 1), key_gain[i], 0.0)

    loop(0, share, put_gain)
    if z_count > 1:
        loop(
            1, z_count,
            lambda d: remote(
                gs, gz.at[z], gain_send.at[0], gain_recv.at[0], {"grp": x * z_count + lax.rem(z + d, z_count)}
            ).start(),
        )
    def code_of(index, slot):
        at = (grp + (0, -1, 1)[slot]) * frames + index
        inside = (at >= 0) & (at < frames * group_count)
        own_clip = clip[lax.rem(at + frames * group_count, frames * group_count)]
        return jnp.where(inside, own_clip, -1), jnp.where(inside, count[own_clip], 0)

    col, row = iota((3 * wide, 1), 0), iota((1, 3 * wide), 1)
    col_code, row_code = jnp.zeros((3 * wide, 1), jnp.int32), jnp.zeros((1, 3 * wide), jnp.int32)
    col_count = jnp.zeros((3 * wide, 1), jnp.int32)
    for slot in range(3):
        def put_code(i, carry, slot=slot):
            col_code, row_code, col_count = carry
            code, most = code_of(i, slot)

            def here(index):
                return (lax.div(index, wide) == slot) & (lax.rem(index, frames) == i)

            return (
                jnp.where(here(col), code, col_code),
                jnp.where(here(row), code, row_code),
                jnp.where(here(col), most, col_count),
            )

        col_code, row_code, col_count = lax.fori_loop(0, frames, put_code, (col_code, row_code, col_count))

    def position(index):
        return lax.div(lax.rem(index, wide), frames)

    bias[...] = jnp.where((col_code == row_code) & (position(col) == position(row)), 0.0, NEGATIVE)
    limit[...] = col_count - position(col)
    down, across = iota((rows, rows), 0), iota((rows, rows), 1)
    for i, (one, other) in enumerate(((down, across), (across, down))):
        source = lax.rem(one, frames) * POS + lax.div(one, frames)
        perms[i] = jnp.where(source == other, 1.0, 0.0).astype(bf16)

    gz[z] = gs[...]
    if z_count > 1:
        wait_bytes(gz.at[pl.ds(0, z_count - 1)], gain_recv.at[0])
        wait_bytes(gz.at[pl.ds(0, z_count - 1)], gain_send.at[0])
    gs[...] = jnp.sum(gz[...], axis=0)
    loop(
        1, X,
        lambda d: remote(
            gs, gx.at[x], gain_send.at[1], gain_recv.at[1], {"grp": lax.rem(x + d, X) * z_count + z}
        ).start(),
    )
    gx[x] = gs[...]

    def halo(c, way):
        return remote(
            win.at[c, 0], win.at[c, 1 + way], halo_send.at[c, way], halo_recv.at[c, way],
            {"grp": lax.rem(grp + (1, group_count - 1)[way], group_count)},
        )

    def to_neighbours(c):
        wait_bytes(win.at[c, 0], recv_sem.at[c])
        for way in range(2):
            halo(c, way).start()

    def attend(c, between):
        lanes_of = [slice(h * HEAD_DIM, (h + 1) * HEAD_DIM) for h in range(CHUNK_HEADS)]
        gain_of = [
            [gains[a : a + 1, c * CH + h * HEAD_DIM : c * CH + (h + 1) * HEAD_DIM] for a in range(2)]
            for h in range(CHUNK_HEADS)
        ]

        def gather(slot):
            for a in range(4):
                moved = dot(perms[0], win[c, slot, a].reshape(rows, CH), ((1,), (0,)))
                for h in range(CHUNK_HEADS):
                    part = moved[:, lanes_of[h]]
                    if a < 2:
                        inverse = lax.rsqrt(mean_lanes(part * part) + EPS)
                        normed[a, h, slot] = (part * inverse * gain_of[h][a]).astype(bf16)

                        if isinstance(slot, int):
                            held[a, h] = part
                    else:
                        normed[a, h, slot] = part.astype(bf16)

        gather(0)
        for way in range(2):
            halo(c, way).wait_recv()
        loop(1, 3, gather)
        between[0]()

        def block(b, sums):
            at = pl.ds(pl.multiple_of(b * wide, wide), wide)
            live = jnp.where(limit[...] > y * POS + b * BLOCK_POS, 1.0, 0.0)
            new = []
            for h in range(CHUNK_HEADS):
                query, key, value, cotangent = (
                    normed[a, h, :, at, :].reshape(3 * wide, HEAD_DIM) for a in range(4)
                )
                scores = dot(query, key, ((1,), (1,))) * SCALE + bias[...]
                prob_grad = dot(cotangent, value, ((1,), (1,)))
                spread = jnp.exp(scores - jnp.max(scores, axis=-1, keepdims=True))
                probs = spread * (live / jnp.sum(spread, axis=-1, keepdims=True))
                rounded = probs.astype(bf16)
                attended = dot(rounded, value, ((1,), (0,))).astype(bf16)
                delta = jnp.sum(cotangent.astype(f32) * attended.astype(f32), axis=-1, keepdims=True)
                score_grad = (probs * (prob_grad - delta) * SCALE).astype(bf16)
                back[0, at, lanes_of[h]] = attended[:wide]
                back[3, at, lanes_of[h]] = dot(rounded[:, :wide], cotangent, ((0,), (0,))).astype(bf16)
                ups = (
                    dot(score_grad[:wide], key, ((1,), (0,))),
                    dot(score_grad[:, :wide], query, ((0,), (0,))),
                )
                for a in range(2):
                    up = ups[a].astype(bf16).astype(f32)
                    rows_in = held[a, h, at, :]
                    inverse = lax.rsqrt(mean_lanes(rows_in * rows_in) + EPS)
                    weighted = up * gain_of[h][a]
                    along = mean_lanes(weighted * rows_in)
                    scaled = rows_in * inverse
                    back[1 + a, at, lanes_of[h]] = (
                        inverse * weighted - scaled * inverse * inverse * along
                    ).astype(bf16)
                    new.append(sums[len(new)] + jnp.sum(up * scaled, axis=0, keepdims=True))
            return tuple(new)

        zero = jnp.zeros((1, HEAD_DIM), f32)
        sums = lax.fori_loop(0, POS // BLOCK_POS, block, (zero,) * (2 * CHUNK_HEADS))
        between[1]()
        for a in range(4):
            out = dot(perms[1], back[a], ((1,), (0,))).astype(bf16).reshape(frames, POS, CH)
            if a == 0:
                att[c, pl.ds(0, frames)] = out
            else:
                ret[c, a - 1] = out
        at_row = iota((POS, CH), 0)
        packed = jnp.zeros((POS, CH), f32)
        for a in range(2):
            packed = packed + hi_lo(jnp.concatenate(sums[a::2], axis=1), at_row, 2 * a)
        att[c, frames] = packed.astype(bf16)

    neighbours = (lax.rem(y + 1, y_count) * CORES + core, lax.rem(y + y_count - 1, y_count) * CORES + core)
    sibling = y * CORES + 1 - core
    first_part = (frames + 1) // 2
    halves = ((0, first_part), (first_part, frames + 1 - first_part))

    def ring_copy(c, way, hop, ref=None):
        at = lax.rem(y + hop * (y_count - 1 if way == 0 else 1), y_count)
        src, dst = ag.at[c, core, at], ag.at[c, core, at]
        if ref is not None:
            src = ref
        if hop + 1 == far:
            src, dst = src.at[pl.ds(*halves[way])], dst.at[pl.ds(*halves[way])]
        return remote(src, dst, ring_send.at[c, way, hop], ring_recv.at[c, way, hop], {"seq": neighbours[way]})

    def to_sibling(c, src, dst):
        remote(src, dst, sib_send.at[c], sib_recv.at[c], {"seq": sibling}).start()

    def ring_step(c, hop):
        for way in range(2):
            at = lax.rem(y + (hop + 1) * (y_count - 1 if way == 0 else 1), y_count)
            ref = ag.at[c, core, at]
            if hop + 1 == far:
                ref = ref.at[pl.ds(*halves[way])]
            wait_bytes(ref, ring_recv.at[c, way, hop])
            if hop + 1 < far:
                ring_copy(c, way, hop + 1).start()
            to_sibling(c, ref, ref)

    def ring_start(c):
        for way in range(2):
            ring_copy(c, way, 0, att.at[c]).start()
        to_sibling(c, att.at[c], ag.at[c, core, y])
        pltpu.make_async_copy(att.at[c], ag.at[c, core, y], own_sem.at[c]).start()

    def give_back(c, low, high):
        mine = rows_out.at[pl.ds(0, 3), y, :, pl.ds(pl.multiple_of(core * HALF + c * CH, HEAD_DIM), CH)]

        def send(i):
            odd = lax.rem(i, 2)
            other = lax.rem(seq + odd * lax.div(i + 1, 2) + (1 - odd) * (seq_count - lax.div(i, 2)), seq_count)
            remote(ret.at[c, :, other], mine, ret_send.at[c], ret_recv, {"seq": other}).start()

        if low == 0:
            pltpu.make_async_copy(ret.at[c, :, seq], mine, ret_recv).start()
        loop(max(low, 1), high, send)

    units = 2 * z_count
    turn[...] = jnp.zeros_like(turn)

    def weigh(c):
        wait_bytes(ag.at[c, core, y], own_sem.at[c])
        wait_bytes(ag.at[c, 1 - core], sib_recv.at[c])
        for kc in range(CORES):
            pltpu.make_async_copy(
                ag.at[c, kc, :, seq], rows_out.at[3, :, :, pl.ds(kc * HALF + c * CH, CH)], ret_recv
            ).start()
            right = jnp.concatenate([ag[c, kc, :, f].reshape(patches, CH) for f in range(frames)], axis=0)
            turn[pl.ds(0, width)] = dot(tokens[...], right, ((1,), (0,)))
            terms = jnp.sum(ag[c, kc, :, frames].astype(f32), axis=0)
            at_row = iota((POS, CH), 0)
            packed = hi_lo(terms[0:1] + terms[1:2], at_row, 0) + hi_lo(terms[2:3] + terms[3:4], at_row, 2)
            turn[pl.ds(width, POS)] = packed
            zall[kc, pl.ds(c * CH, CH)] = turn[...].T.astype(bf16)
        for unit in range(units * c // CHUNKS, units * (c + 1) // CHUNKS):
            for kc in range(CORES):
                owner = (2 * kc + unit // z_count) * z_count + unit % z_count

                @pl.when(grp != owner)
                def _(kc=kc, unit=unit, owner=owner):
                    remote(
                        zall.at[kc, pl.ds(unit * share, share)], shares.at[grp], share_send, share_recv, {"grp": owner}
                    ).start()

    def project():
        def frame_pair(i):
            left = jnp.concatenate(
                [
                    jnp.concatenate(
                        [ag[c, kc, :, 2 * i + j].reshape(patches, CH) for kc in range(CORES) for c in range(CHUNKS)], axis=1
                    )
                    for j in range(2)
                ],
                axis=0,
            )
            total = dot(w[...], left, ((1,), (1,))).astype(bf16)
            for j in range(2):
                proj_out[2 * i + j] = total[:, j * patches : (j + 1) * patches]

        loop(0, frames // 2, frame_pair)

    def part(eighths):
        return seq_count * eighths // 8

    def drain(c):
        wait_bytes(win.at[c, 0, :, pl.ds(0, seq_count - 1)], send_sem.at[c])
        for way in range(2):
            halo(c, way).wait_send()
            for hop in range(far):
                ring_copy(c, way, hop).wait_send()
        wait_bytes(ag.at[c, core], sib_send.at[c])
        wait_bytes(ret.at[c, :, pl.ds(0, seq_count - 1)], ret_send.at[c])

    def run(*events):
        def go():
            for event, c, *more in events:
                if event == "step" and more[0] < far:
                    ring_step(c, *more)
                elif event == "ring":
                    ring_start(c)
                elif event == "ret":
                    give_back(c, part(more[0]), part(more[1]))
                elif event == "weigh":
                    weigh(c)

        return go

    nothing = run()
    to_neighbours(0)
    wait_bytes(gx.at[pl.ds(0, X - 1)], gain_recv.at[1])
    gains[...] = jnp.sum(gx[...], axis=0)
    to_neighbours(1)
    attend(0, (nothing, nothing))
    run(("ring", 0), ("ret", 0, 0, 8))()
    to_neighbours(2)
    attend(1, (run(("step", 0, 0)), nothing))
    run(("ring", 1), ("step", 0, 1))()
    attend(2, (run(("step", 0, 2), ("step", 1, 0)), run(("ret", 1, 0, 3), ("step", 0, 3))))
    run(("ring", 2), ("step", 1, 1), ("ret", 1, 3, 5), ("step", 2, 0))()
    for load in (pltpu.make_async_copy(tokens, tokens, load_sem.at[4]), pltpu.make_async_copy(weight, w, load_sem.at[5])):
        load.wait()
    run(("weigh", 0), ("ret", 1, 5, 6), ("step", 1, 2), ("step", 2, 1), ("ret", 1, 6, 8), ("step", 1, 3), ("weigh", 1), ("step", 2, 2), ("ret", 2, 0, 4), ("step", 2, 3), ("weigh", 2), ("ret", 2, 4, 8))()
    project()
    for c in range(CHUNKS - 1):
        drain(c)
    wait_bytes(gx.at[pl.ds(0, X - 1)], gain_send.at[1])
    own_unit = lax.rem(x, 2) * z_count + z
    shares[grp] = zall[lax.div(x, 2), pl.ds(pl.multiple_of(own_unit * share, POS), share)]
    wait_bytes(shares.at[pl.ds(0, group_count - 1)], share_recv)
    token_root = float(frames * patches * group_count) ** 0.5
    total = jnp.sum(shares[...].astype(f32), axis=0) / token_root
    wide_out[...] = total[:, :width]
    terms = total.T
    gain_out[0:1] = terms[width : width + 1] + terms[width + 1 : width + 2]
    gain_out[1:2] = terms[width + 2 : width + 3] + terms[width + 3 : width + 4]
    drain(CHUNKS - 1)
    wait_bytes(shares.at[pl.ds(0, group_count - 1)], share_send)
    wait_bytes(rows_out, ret_recv)


def hand_out_kernel(rows_in, proj_in, wide_in, gain_in, *rest):
    outs, sem = rest[:-1], rest[-1]
    parts = [(rows_in.at[i], outs[i]) for i in range(4)] + [(proj_in, outs[4])]
    copies = []
    for src, dst in parts:
        half = src.shape[0] // 2
        for low in (0, half):
            at = pl.ds(low, half)
            copies.append(pltpu.make_async_copy(src.at[at], dst.at[at], sem.at[len(copies)]))
    for copy in copies:
        copy.start()
    outs[5][...] = wide_in[...]
    for i in range(2):
        outs[6 + i][...] = gain_in[i]
    for copy in copies:
        copy.wait()


def body(
    query_rows,
    key_rows,
    value_rows,
    out_grad,
    proj_grad,
    proj_weight,
    query_gain,
    key_gain,
    clip_of_frame,
    patch_count,
):
    bf16, f32 = jnp.bfloat16, jnp.float32
    patches, channels = query_rows.shape[1:]
    seq_count, group_count = lax.axis_size("seq"), lax.axis_size("grp")
    y_count, z_count = seq_count // CORES, group_count // X
    frames = seq_count
    width = proj_weight.shape[0]
    share = channels // group_count
    rows = frames * POS
    wide = BLOCK_POS * frames
    far = y_count // 2
    vmem, anywhere = pl.BlockSpec(memory_space=pltpu.VMEM), pl.BlockSpec(memory_space=pl.ANY)
    dma = pltpu.SemaphoreType.DMA
    rows_out, projected, wide_out, gain_out = pl.pallas_call(
        fused_kernel,
        out_shape=(
            jax.ShapeDtypeStruct((4, y_count, POS, channels), bf16),
            jax.ShapeDtypeStruct((frames, width, patches), bf16),
            jax.ShapeDtypeStruct((share, width), f32),
            jax.ShapeDtypeStruct((2, share), f32),
        ),
        in_specs=[pl.BlockSpec(memory_space=pltpu.HBM)] * 10,
        out_specs=(anywhere, vmem, vmem, vmem),
        scratch_shapes=[
            pltpu.VMEM((4, y_count, POS, channels), bf16),
            pltpu.VMEM((CHUNKS, 3, 4, frames, POS, CH), bf16),
            pltpu.VMEM((4, CHUNK_HEADS, 3, rows, HEAD_DIM), bf16),
            pltpu.VMEM((2, CHUNK_HEADS, rows, HEAD_DIM), f32),
            pltpu.VMEM((3 * wide, 3 * wide), f32),
            pltpu.VMEM((3 * wide, 1), jnp.int32),
            pltpu.VMEM((2, rows, rows), bf16),
            pltpu.VMEM((4, rows, CH), bf16),
            pltpu.VMEM((CHUNKS, 3, frames, POS, CH), bf16),
            pltpu.VMEM((CHUNKS, frames + 1, POS, CH), bf16),
            pltpu.VMEM((CHUNKS, CORES, y_count, frames + 1, POS, CH), bf16),
            pltpu.VMEM((width, frames * patches), bf16),
            pltpu.VMEM((width, channels), bf16),
            pltpu.VMEM((LANES, CH), f32),
            pltpu.VMEM((CORES, HALF, LANES), bf16),
            pltpu.VMEM((group_count, share, LANES), bf16),
            pltpu.VMEM((z_count, 8, HALF), f32),
            pltpu.VMEM((X, 8, HALF), f32),
            pltpu.VMEM((8, HALF), f32),
            pltpu.VMEM((8, HALF), f32),
            pltpu.SMEM((share,), f32),
            pltpu.SMEM((share,), f32),
            pltpu.SMEM(clip_of_frame.shape, jnp.int32),
            pltpu.SMEM(patch_count.shape, jnp.int32),
            dma((10,)),
            dma((CHUNKS,)),
            dma((CHUNKS,)),
            dma((CHUNKS, 2)),
            dma((CHUNKS, 2)),
            dma((2,)),
            dma((2,)),
            dma((CHUNKS,)),
            dma,
            dma((CHUNKS,)),
            dma((CHUNKS, 2, far)),
            dma((CHUNKS, 2, far)),
            dma((CHUNKS,)),
            dma((CHUNKS,)),
            dma,
            dma,
        ],
        compiler_params=pltpu.CompilerParams(collective_id=0, has_side_effects=True, vmem_limit_bytes=VMEM_LIMIT),
        name="fused",
    )(
        *(
            pltpu.with_memory_space_constraint(a, pltpu.HBM)
            for a in (
                *(a.reshape(y_count, POS, channels) for a in (query_rows, key_rows, value_rows, out_grad)),
                query_gain, key_gain, clip_of_frame, patch_count, proj_grad, proj_weight,
            )
        )
    )
    by_position = jax.ShapeDtypeStruct((y_count, POS, channels), bf16)
    outs = pl.pallas_call(
        hand_out_kernel,
        out_shape=(by_position,) * 4
        + (
            jax.ShapeDtypeStruct(projected.shape, bf16),
            jax.ShapeDtypeStruct(wide_out.shape, f32),
            jax.ShapeDtypeStruct((share,), f32),
            jax.ShapeDtypeStruct((share,), f32),
        ),
        in_specs=[vmem] * 4,
        out_specs=(anywhere,) * 5 + (vmem,) * 3,
        scratch_shapes=[dma((10,))],
        compiler_params=pltpu.CompilerParams(vmem_limit_bytes=VMEM_LIMIT),
        name="hand_out",
    )(rows_out, projected, wide_out, gain_out)
    query_grad, key_grad, value_grad, attended = (rows.reshape(1, patches, channels) for rows in outs[:4])
    return attended, outs[4], query_grad, key_grad, value_grad, *outs[5:]


def solution(mesh):
    rows = P(("grp", "seq"), None, None)
    in_specs = (rows, rows, rows, rows, P("grp", "seq", None), P("seq", None), P("grp"), P("grp"), P(), P())
    out_specs = (rows, P("grp", "seq", None), rows, rows, rows, P("grp", "seq"), P("grp"), P("grp"))
    return jax.shard_map(body, mesh=mesh, in_specs=in_specs, out_specs=out_specs, check_vma=False)
```
